256 devices in a mesh: rup: 16 (over x, z_hi), site: 16 (over z_lo, y, core).
Axes of the slice: x: 4, y: 4, z: 8 (z_hi: 4, z_lo: 2; z = z_hi * 2 + z_lo), core: 2. Of those that a mesh axis runs over, the one named last changes fastest.
Arguments:
- site_x: float32 [65536], P('site'), may hold values from 0 to 100
- site_y: float32 [65536], P('site'), may hold values from 0 to 100
- site_amp: float32 [65536], P('site'), may hold values from -1.2 to 1.2
- rup_x: float32 [2048], P('rup'), may hold values from 0 to 100
- rup_y: float32 [2048], P('rup'), may hold values from 0 to 100
- rup_mag: float32 [2048], P('rup'), may hold values from 5 to 8
- rup_rate: float32 [2048], P('rup'), may hold values from 0.0002 to 0.012
- rup_source: int32 [2048], P('rup'), may hold values from 0 to 63
- src_sigma: float32 [64], replicated, may hold values from 0.04 to 0.85
- src_shift: float32 [64], replicated, may hold values from -1.6 to 1.6
- relay_sites: int32 [16, 16, 16, 128], P('rup', 'site'), may hold values from 0 to 4095
- relay_count: int32 [16, 16, 16], P('rup', 'site'), may hold values from 1 to 128, 1536 in all within a row
- asset_source: int32 [524288], P(('rup', 'site')), may hold values from 0 to 15
- asset_pick: int32 [524288], P(('rup', 'site')), may hold values from 0 to 16383
- asset_class: int32 [524288], P(('rup', 'site')), may hold values from 0 to 127
- vulnerability: float32 [128, 32, 32], replicated, may hold values from 0 to 1
Outputs:
- hazard: float32 [32, 65536], P(None, 'site')
- losses: float32 [32, 524288], P(None, ('rup', 'site'))
The draws below stay inside these ranges and needn't reach their ends.
Inputs may be any that keep to these rules, and one draw needn't show every extreme that they name: `relay_count`: for each index of rup and each owner, the counts of that owner over its source blocks add up to 3 * 128 * (devices of site) / 4 (the sum is per owner, not over a whole index of rup), and among them some count is exactly 128.
All inputs are finite; a program needn't handle non-finite values.
Results may differ from the reference program's by a relative error of at most 0.00019.
Values sent between devices are 32-bit elements; how exact they have to be, the bound alone decides.
No kernel may reach another device: no remote copies, remote signals or barrier semaphores. Data moves between devices by JAX's collectives and lax.ppermute only.
A program may use at most 128 MiB of HBM per device.

```python
import math
import jax
import jax.numpy as jnp
import numpy as np
from jax import lax

L = 32
LR = 32
NCLASS = 128
NSRC = 64
CAP = 128
SITE_DEV = 4096
ASSET_DEV = 2048
SITES = 65536
RUPTURES = 2048
ASSETS = 524288
N_RUP = 16
N_SITE = 16


def plant(array, key, least, top_value):
    longest = array.shape.index(max(array.shape))
    spots = []
    for shift in (0, 1):
        where = [jax.random.randint(jax.random.fold_in(key, axis), (), 0, length) for axis, length in enumerate(array.shape)]
        where[longest] = (where[longest] + shift) % array.shape[longest]
        spots.append(tuple(where))
    return array.at[spots[0]].set(least).at[spots[1]].set(top_value)


def shard_levels(own_key, extent, cuts, low, high):
    def one(dim, shards_of):
        steps = jax.random.uniform(jax.random.fold_in(jax.random.fold_in(own_key, 6), dim), (shards_of,), jnp.float32, low / len(cuts), high / len(cuts))
        return jnp.repeat(jnp.exp(steps), extent[dim] // shards_of).reshape((-1,) + (1,) * (len(extent) - dim - 1))

    gain = one(*cuts[0])
    for cut in cuts[1:]:
        gain = gain * one(*cut)
    return gain


def cumulative_ranks(count, lean):
    loads = [(1 << 20) // math.isqrt(rank ** lean) + 1 for rank in range(1, count + 1)]
    deviation = 1 + sum(loads) // (1 << 30)
    return np.cumsum(np.array([max(1, weight // deviation) for weight in loads]))


def ranked(stream_key, shape, amount, lean):
    table = cumulative_ranks(amount, lean)
    pick = jax.random.randint(jax.random.fold_in(stream_key, 1), shape, 0, int(table[amount - 1]))
    standing = jnp.searchsorted(jnp.asarray(table, jnp.int32), pick, side="right")
    return jax.random.permutation(jax.random.fold_in(stream_key, 2), amount)[standing].astype(jnp.int32)


def split_up(count, total, reach, skew):
    portions = [(1 << 20) // math.isqrt(standing ** skew) + 1 for standing in range(2, count + 1)]
    rest, counts = total - reach - (count - 1), [1] * (count - 1)
    while rest > 0:
        candidates = [i for i in range(count - 1) if counts[i] < reach]
        whole, left = sum([portions[i] for i in candidates]), rest
        for i in candidates:
            addition = min(reach - counts[i], max(1, left * portions[i] // whole), rest)
            counts[i] = counts[i] + addition
            rest = rest - addition
    return np.array([reach] + counts)


def uneven(rng, count, total, limit, skew):
    if count == 2:
        one = jax.random.randint(rng, (), max(1, total - limit), min(limit, total - 1) + 1)
        return jnp.stack([one, total - one])
    lengths = jnp.asarray(split_up(count, total, limit, skew), jnp.int32)
    twos = (count - 1) // 2
    giver, sink = lengths[1:1 + 2 * twos:2], lengths[2:2 + 2 * twos:2]
    margin = jnp.minimum(giver - 1, limit - sink)
    passed = jax.random.randint(jax.random.fold_in(rng, 1), (twos,), 0, 1 << 20) % (margin + 1)
    lengths = lengths.at[1:1 + 2 * twos:2].set(giver - passed).at[2:2 + 2 * twos:2].set(sink + passed)
    return lengths[jax.random.permutation(jax.random.fold_in(rng, 2), count)]


def gaussian(rng, extent, scale, reach, split=(), kind=jnp.bfloat16):
    result = scale * jax.random.normal(rng, extent, jnp.float32)
    if split:
        result = result * shard_levels(rng, extent, split, -0.22, 0.18)
    return jnp.clip(result, -reach, reach).astype(kind)


def setup_inputs(seed: int = 0) -> dict:
    arg_keys = jax.random.split(jax.random.key(seed), 17)
    site_x = jnp.clip(100.0 * jax.random.uniform(arg_keys[0], (SITES,), jnp.float32) ** shard_levels(arg_keys[0], (SITES,), ((0, 16),), -0.2, 0.2), 0.0, 100.0)
    site_y = jnp.clip(100.0 * jax.random.uniform(arg_keys[1], (SITES,), jnp.float32) ** shard_levels(arg_keys[1], (SITES,), ((0, 16),), -0.2, 0.2), 0.0, 100.0)
    site_amp = gaussian(arg_keys[2], (SITES,), 0.3, 1.2, ((0, 16),), jnp.float32)
    rup_x = jnp.clip(100.0 * jax.random.uniform(arg_keys[3], (RUPTURES,), jnp.float32) ** shard_levels(arg_keys[3], (RUPTURES,), ((0, 16),), -0.2, 0.2), 0.0, 100.0)
    rup_y = jnp.clip(100.0 * jax.random.uniform(arg_keys[4], (RUPTURES,), jnp.float32) ** shard_levels(arg_keys[4], (RUPTURES,), ((0, 16),), -0.2, 0.2), 0.0, 100.0)
    rup_mag = jnp.clip(5.0 + 3.0 * jax.random.uniform(arg_keys[5], (RUPTURES,), jnp.float32) ** shard_levels(arg_keys[5], (RUPTURES,), ((0, 16),), -0.2, 0.2), 5.0, 8.0)
    rup_rate = jnp.clip(jnp.exp(math.log(0.012) - 4.0943446 * jax.random.uniform(arg_keys[6], (RUPTURES,), jnp.float32) ** shard_levels(arg_keys[6], (RUPTURES,), ((0, 16),), -0.2, 0.2)), 0.0002, 0.012)
    rup_source = plant(jax.random.randint(arg_keys[7], (RUPTURES,), 0, NSRC), jax.random.fold_in(arg_keys[7], 1), 0, NSRC - 1).astype(jnp.int32)
    src_sigma = jnp.clip(jnp.exp(jax.random.uniform(arg_keys[8], (NSRC,), jnp.float32, math.log(0.04), math.log(0.85))), 0.04, 0.85)
    src_shift = gaussian(arg_keys[9], (NSRC,), 0.4, 1.6, (), jnp.float32)
    relay_sites = plant(jax.random.randint(arg_keys[10], (N_RUP, N_SITE, N_SITE, CAP), 0, SITE_DEV), jax.random.fold_in(arg_keys[10], 1), 0, SITE_DEV - 1).astype(jnp.int32)
    relay_count = jax.vmap(lambda own: uneven(own, N_SITE, 3 * N_SITE * CAP // 4, CAP, 2))(jax.random.split(arg_keys[11], N_RUP * N_SITE)).reshape((N_RUP, N_SITE, N_SITE)).astype(jnp.int32)
    asset_source = plant(jax.random.randint(arg_keys[12], (ASSETS,), 0, N_SITE), jax.random.fold_in(arg_keys[12], 1), 0, N_SITE - 1).astype(jnp.int32)
    asset_pick = plant(jax.random.randint(arg_keys[13], (ASSETS,), 0, 16384), jax.random.fold_in(arg_keys[13], 1), 0, 16383).astype(jnp.int32)
    asset_class = plant(ranked(arg_keys[14], (ASSETS,), NCLASS, 2), jax.random.fold_in(arg_keys[14], 3), 0, NCLASS - 1).astype(jnp.int32)
    vulnerability = jnp.clip(jax.random.uniform(arg_keys[15], (NCLASS, L, LR), jnp.float32, 0.0, 1.0), 0.0, 1.0)
    return {"site_x": site_x, "site_y": site_y, "site_amp": site_amp, "rup_x": rup_x, "rup_y": rup_y, "rup_mag": rup_mag, "rup_rate": rup_rate, "rup_source": rup_source, "src_sigma": src_sigma, "src_shift": src_shift, "relay_sites": relay_sites, "relay_count": relay_count, "asset_source": asset_source, "asset_pick": asset_pick, "asset_class": asset_class, "vulnerability": vulnerability}


def log_levels(count):
    position = jnp.arange(count, dtype=jnp.float32)
    return math.log(0.005) + position * (math.log(600.0) / (count - 1))

def block_size(length, preferred):
    return preferred if length % preferred == 0 else length

def exceed_rates(north_pos, east_pos, amplify, rup_x, rup_y, median_base, spread, rup_rate, levels):
    delta_x = north_pos[None, :] - rup_x[:, None]
    delta_y = east_pos[None, :] - rup_y[:, None]
    median = median_base[:, None] + amplify[None, :] - 0.6 * jnp.log((delta_x * delta_x + delta_y * delta_y + 100.0) / 100.0)
    scaled = (levels[:, None, None] - median[None, :, :]) / (spread[None, :, None] * math.sqrt(2.0))
    chance = 0.5 * lax.erfc(scaled)
    return lax.optimization_barrier(jnp.sum(chance * rup_rate[None, :, None], axis=1))

def reference(site_x, site_y, site_amp, rup_x, rup_y, rup_mag, rup_rate, rup_source, src_sigma, src_shift, relay_sites, relay_count, asset_source, asset_pick, asset_class, vulnerability):
    levels = log_levels(L)
    median_base = -1.0 + (rup_mag - 6.5) + src_shift[rup_source]
    spread = src_sigma[rup_source]
    site_block = block_size(SITES, 256)
    blocks = SITES // site_block

    def one_block(pieces):
        return exceed_rates(pieces[0], pieces[1], pieces[2], rup_x, rup_y, median_base, spread, rup_rate, levels)
    rates = lax.map(one_block, (site_x.reshape(blocks, site_block), site_y.reshape(blocks, site_block), site_amp.reshape(blocks, site_block)))
    rates = jnp.moveaxis(rates, 1, 0).reshape(L, SITES)
    hazard = 1.0 - jnp.exp(-rates)
    asset_index = jnp.arange(ASSETS, dtype=jnp.int32)
    device_index = asset_index // ASSET_DEV
    row_index = device_index // N_SITE
    owner_index = device_index % N_SITE
    source_count = relay_count[row_index, owner_index, asset_source]
    local_site = relay_sites[row_index, owner_index, asset_source, asset_pick % source_count]
    asset_site = (asset_source * SITE_DEV + local_site).astype(jnp.int32)
    curves = hazard[:, asset_site]
    occurrence = curves - jnp.concatenate([curves[1:], jnp.zeros((1, ASSETS), jnp.float32)], axis=0)
    asset_block = block_size(ASSETS, 2048)
    nblocks = ASSETS // asset_block

    def block_losses(pieces):
        occur_part, class_part = pieces
        chosen = vulnerability[class_part]
        return jnp.einsum('la,alm->ma', occur_part, chosen, precision=lax.Precision.HIGHEST)
    loss_parts = lax.map(block_losses, (jnp.moveaxis(occurrence.reshape(L, nblocks, asset_block), 1, 0), asset_class.reshape(nblocks, asset_block)))
    losses = jnp.moveaxis(loss_parts, 0, 1).reshape(LR, ASSETS)
    return (hazard, losses)
```

```python
import functools
import math

import jax
import jax.numpy as jnp
from jax import lax
from jax.experimental import pallas as pl
from jax.experimental.pallas import tpu as pltpu
from jax.sharding import PartitionSpec as P

LANES = 128
SUBLANES = 8
VMEM = pl.BlockSpec(memory_space=pltpu.VMEM)
SMEM = pl.BlockSpec(memory_space=pltpu.SMEM)
LEVEL_FIRST = math.log(0.005)
LEVEL_RANGE = math.log(600.0)


def lane_gather(row, index):
    return jnp.take_along_axis(row, index, axis=1, mode="promise_in_bounds")


def pack_kernel(x_ref, y_ref, mag_ref, rate_ref, source_ref, sigma_ref, shift_ref, out_ref):
    sources = sigma_ref.shape[1]
    index = jnp.broadcast_to(source_ref[...], (SUBLANES, LANES))
    pad = jnp.zeros((1, LANES - sources), jnp.float32)
    sigma = jnp.broadcast_to(jnp.concatenate([sigma_ref[...], pad], axis=1), (SUBLANES, LANES))
    shift = jnp.broadcast_to(jnp.concatenate([shift_ref[...], pad], axis=1), (SUBLANES, LANES))
    spread = lane_gather(sigma, index)[0:1]
    base = -1.0 + (mag_ref[...] - 6.5) + lane_gather(shift, index)[0:1]
    inverse = 1.0 / (spread * math.sqrt(2.0))
    zero = jnp.zeros((1, LANES), jnp.float32)
    packed = jnp.concatenate(
        [x_ref[...], y_ref[...], base, inverse, 0.5 * rate_ref[...], zero, zero, zero], axis=0
    )
    for peer in range(out_ref.shape[0]):
        out_ref[peer] = packed


def hazard_kernel(levels, row_ref, sx_ref, sy_ref, amp_ref, rup_ref, out_ref, col_ref, start_ref):
    blocks = rup_ref.shape[0]
    ruptures = blocks * LANES
    tiles = out_ref.shape[1] // LANES
    row = row_ref[0] * tiles
    step = LEVEL_RANGE / (levels - 1)
    for b in range(blocks):
        packed = rup_ref[b]
        square = jnp.concatenate(
            [packed, jnp.zeros((LANES - SUBLANES, LANES), jnp.float32)], axis=0
        )
        columns = jnp.transpose(square)
        for p in range(5):
            col_ref[p, b * LANES : (b + 1) * LANES, :] = jnp.broadcast_to(
                columns[:, p : p + 1], (LANES, LANES)
            )
    unroll = 8
    rows = unroll * SUBLANES
    for t in range(tiles):
        site_x = sx_ref[pl.ds(row + t, 1), :]
        site_y = sy_ref[pl.ds(row + t, 1), :]
        amp = amp_ref[pl.ds(row + t, 1), :]

        def prepare(g, carry):
            at = pl.ds(pl.multiple_of(g * rows, rows), rows)
            dx = site_x - col_ref[0, at, :]
            dy = site_y - col_ref[1, at, :]
            median = col_ref[2, at, :] + amp - 0.6 * jnp.log((dx * dx + dy * dy + 100.0) / 100.0)
            start_ref[t, at, :] = (LEVEL_FIRST - median) * col_ref[3, at, :]
            return carry

        lax.fori_loop(0, ruptures // rows, prepare, 0)

    half = levels // 2
    for t in range(tiles):
        for first in range(0, levels, half):

            def body(g, acc):
                acc = list(acc)
                for u in range(unroll):
                    at = pl.ds(pl.multiple_of(g * rows + u * SUBLANES, SUBLANES), SUBLANES)
                    gap = col_ref[3, at, :] * step
                    rate = col_ref[4, at, :]
                    z = start_ref[t, at, :]
                    if first:
                        z = z + gap * float(first)
                    for l in range(half):
                        acc[l] = acc[l] + rate * (1.0 - lax.erf(z))
                        z = z + gap
                return tuple(acc)

            zero = jnp.zeros((SUBLANES, LANES), jnp.float32)
            acc = lax.fori_loop(0, ruptures // rows, body, (zero,) * half)
            for l in range(half):
                rates = jnp.sum(acc[l], axis=0, keepdims=True)
                out_ref[pl.ds(first + l, 1), t * LANES : (t + 1) * LANES] = 1.0 - jnp.exp(-rates)


def relay_kernel(blocks_ref, index_ref, hazard_ref, send_ref):
    blocks, levels, width = blocks_ref.shape
    owners = index_ref.shape[0]
    groups = levels // SUBLANES
    tiles = width // LANES
    for b in range(blocks):
        hazard_ref[:, b * width : (b + 1) * width] = blocks_ref[b]

    def one_owner(d, carry):
        index = jnp.broadcast_to(index_ref[pl.ds(d, 1), :], (SUBLANES, LANES))
        lane = index & (LANES - 1)
        tile = index >> 7
        picked = [jnp.zeros((SUBLANES, LANES), jnp.float32)] * groups
        for c in range(blocks * tiles):
            b, t = c // tiles, c % tiles
            here = tile == c
            for q in range(groups):
                part = blocks_ref[b, q * SUBLANES : (q + 1) * SUBLANES, t * LANES : (t + 1) * LANES]
                picked[q] = jnp.where(here, lane_gather(part, lane), picked[q])
        for q in range(groups):
            send_ref[d, q * SUBLANES : (q + 1) * SUBLANES, :] = picked[q]
        return carry

    lax.fori_loop(0, owners, one_owner, 0)


def loss_kernel(
    curves_ref, source_ref, pick_ref, class_ref, count_ref, table_ref, out_ref, split_ref
):
    sources, levels, _ = curves_ref.shape
    bins = out_ref.shape[0]
    classes = table_ref.shape[1]
    groups = levels // SUBLANES
    assets = out_ref.shape[1]
    source = source_ref[...]
    count = jnp.zeros(source.shape, jnp.int32)
    for s in range(sources):
        count = jnp.where(source == s, count_ref[0, s], count)
    pick = pick_ref[...]
    count_f = count.astype(jnp.float32)
    quotient = jnp.floor(pick.astype(jnp.float32) / count_f).astype(jnp.int32)
    slot = pick - quotient * count
    slot = jnp.where(slot < 0, slot + count, slot)
    slot = jnp.where(slot >= count, slot - count, slot)
    table = table_ref[...]
    high = table.astype(jnp.bfloat16)
    low = (table - high.astype(jnp.float32)).astype(jnp.bfloat16)
    split_ref[:, 0:classes] = high
    split_ref[:, classes : 2 * classes] = low
    width = 2 * LANES
    for t in range(assets // width):
        curve = []
        for h in range(width // LANES):
            i = t * (width // LANES) + h
            lane = jnp.broadcast_to(slot[i : i + 1, :], (SUBLANES, LANES))
            which = jnp.broadcast_to(source[i : i + 1, :], (SUBLANES, LANES))
            picked = [jnp.zeros((SUBLANES, LANES), jnp.float32)] * groups
            for s in range(sources):
                here = which == s
                for q in range(groups):
                    part = curves_ref[s, q * SUBLANES : (q + 1) * SUBLANES, :]
                    picked[q] = jnp.where(here, lane_gather(part, lane), picked[q])
            curve.append(jnp.concatenate(picked, axis=0))
        curves = jnp.concatenate(curve, axis=1)
        following = jnp.concatenate([curves[1:], jnp.zeros((1, width), jnp.float32)], axis=0)
        occurrence = curves - following
        kinds = jnp.concatenate(
            [class_ref[t * (width // LANES) + h : t * (width // LANES) + h + 1, :] for h in range(width // LANES)],
            axis=1,
        )
        match = lax.broadcasted_iota(jnp.int32, (classes, width), 0) == kinds
        onehot = jnp.where(match, 1.0, 0.0).astype(jnp.bfloat16)
        both = jnp.concatenate([onehot, onehot], axis=0)
        chosen = jnp.dot(split_ref[...], both, preferred_element_type=jnp.float32)
        total = jnp.zeros((bins, width), jnp.float32)
        for l in range(levels):
            total = total + occurrence[l : l + 1, :] * chosen[l * bins : (l + 1) * bins, :]
        out_ref[:, t * width : (t + 1) * width] = total


def per_device(
    site_x,
    site_y,
    site_amp,
    rup_x,
    rup_y,
    rup_mag,
    rup_rate,
    rup_source,
    src_sigma,
    src_shift,
    relay_sites,
    relay_count,
    asset_source,
    asset_pick,
    asset_class,
    vulnerability,
    rows,
):
    classes, levels, bins = vulnerability.shape
    sites = site_x.shape[0]
    sources, capacity = relay_sites.shape[2:]
    assets = asset_source.shape[0]
    own_sites = sites // rows
    limit = pltpu.CompilerParams(vmem_limit_bytes=48 * 2**20)

    wanted = lax.all_to_all(relay_sites[0, 0], "site", 0, 0, tiled=True)
    line = lambda a: a.reshape(1, -1)
    packed = pl.pallas_call(
        pack_kernel,
        out_shape=jax.ShapeDtypeStruct((rows, SUBLANES, LANES), jnp.float32),
        in_specs=[VMEM] * 7,
        out_specs=VMEM,
    )(
        line(rup_x),
        line(rup_y),
        line(rup_mag),
        line(rup_rate),
        line(rup_source),
        line(src_sigma),
        line(src_shift),
    )
    ruptures = lax.all_to_all(packed, "rup", 0, 0, tiled=True)
    row = lax.axis_index("rup").astype(jnp.int32).reshape(1)
    square = lambda a: a.reshape(-1, LANES)
    own = pl.pallas_call(
        functools.partial(hazard_kernel, levels),
        out_shape=jax.ShapeDtypeStruct((levels, own_sites), jnp.float32),
        in_specs=[SMEM] + [VMEM] * 4,
        out_specs=VMEM,
        scratch_shapes=[
            pltpu.VMEM((5, rows * LANES, LANES), jnp.float32),
            pltpu.VMEM((own_sites // LANES, rows * LANES, LANES), jnp.float32),
        ],
        compiler_params=limit,
    )(row, square(site_x), square(site_y), square(site_amp), ruptures)
    spread = jnp.broadcast_to(own[None], (rows, levels, own_sites))
    blocks = lax.all_to_all(spread, "rup", 0, 0, tiled=True)
    hazard, send = pl.pallas_call(
        relay_kernel,
        out_shape=(
            jax.ShapeDtypeStruct((levels, sites), jnp.float32),
            jax.ShapeDtypeStruct((sources, levels, capacity), jnp.float32),
        ),
        in_specs=[VMEM] * 2,
        out_specs=(VMEM, VMEM),
        compiler_params=limit,
    )(blocks, wanted)
    curves = lax.all_to_all(send, "site", 0, 0, tiled=True)
    table = jnp.transpose(vulnerability, (1, 2, 0)).reshape(levels * bins, classes)
    losses = pl.pallas_call(
        loss_kernel,
        out_shape=jax.ShapeDtypeStruct((bins, assets), jnp.float32),
        in_specs=[VMEM] * 4 + [SMEM, VMEM],
        out_specs=VMEM,
        scratch_shapes=[pltpu.VMEM((levels * bins, 2 * classes), jnp.bfloat16)],
        compiler_params=limit,
    )(
        curves,
        square(asset_source),
        square(asset_pick),
        square(asset_class),
        relay_count.reshape(1, sources),
        table,
    )
    return hazard, losses


def solution(mesh):
    return jax.shard_map(
        functools.partial(per_device, rows=mesh.shape["rup"]),
        mesh=mesh,
        in_specs=(
            P("site"),
            P("site"),
            P("site"),
            P("rup"),
            P("rup"),
            P("rup"),
            P("rup"),
            P("rup"),
            P(),
            P(),
            P("rup", "site", None, None),
            P("rup", "site", None),
            P(("rup", "site")),
            P(("rup", "site")),
            P(("rup", "site")),
            P(),
        ),
        out_specs=(P(None, "site"), P(None, ("rup", "site"))),
        check_vma=False,
    )
```

```python
import functools
import math

import jax
import jax.numpy as jnp
from jax import lax
from jax.experimental import pallas as pl
from jax.experimental.pallas import tpu as pltpu
from jax.sharding import PartitionSpec as P

LANES = 128
SUBLANES = 8
LIST = 5
PRODUCTS = 2
VMEM = pl.BlockSpec(memory_space=pltpu.VMEM)
SMEM = pl.BlockSpec(memory_space=pltpu.SMEM)
LEVEL_FIRST = math.log(0.005)
LEVEL_RANGE = math.log(600.0)


def lane_gather(row, index):
    return jnp.take_along_axis(row, index, axis=1, mode="promise_in_bounds")


def partner(row, site, other):
    inner = lambda r: (((r & 3) + 1) >> 1) & 1
    south = lambda r: 2 * inner(r) - (r >> 2)
    z_lo = (site >> 3) ^ inner(row) ^ inner(other)
    y = (((site >> 1) & 3) - south(row) + south(other)) & 3
    core = (site & 1) ^ ((row & 3) >> 1) ^ ((other & 3) >> 1)
    return z_lo * 8 + y * 2 + core


def place():
    return lax.axis_index("rup"), lax.axis_index("site")


def split_in_three(value):
    high = value.astype(jnp.bfloat16)
    rest = value - high.astype(jnp.float32)
    middle = rest.astype(jnp.bfloat16)
    return high, middle, (rest - middle.astype(jnp.float32)).astype(jnp.bfloat16)


def pack_kernel(
    x_ref,
    y_ref,
    mag_ref,
    rate_ref,
    source_ref,
    relay_ref,
    sigma_ref,
    shift_ref,
    sx_ref,
    sy_ref,
    amp_ref,
    out_ref,
    own_ref,
):
    row, site = place()
    tiles = sx_ref.shape[0] // out_ref.shape[0]
    for i, ref in enumerate((sx_ref, sy_ref, amp_ref)):
        own_ref[i * tiles : (i + 1) * tiles, :] = ref[pl.ds(row * tiles, tiles), :]
    sources = sigma_ref.shape[1]
    own_ref[3 * tiles : 3 * tiles + 2, :] = jnp.zeros((2, LANES), jnp.float32)
    own_ref[3 * tiles : 3 * tiles + 1, 0:sources] = sigma_ref[...]
    own_ref[3 * tiles + 1 : 3 * tiles + 2, 0:sources] = shift_ref[...]
    source = source_ref[...].astype(jnp.float32)
    zero = jnp.zeros((1, LANES), jnp.float32)
    packed = jnp.concatenate(
        [x_ref[...], y_ref[...], mag_ref[...], rate_ref[...], source, zero, zero, zero], axis=0
    )
    for j in range(out_ref.shape[0]):
        out_ref[j] = packed
        wanted = relay_ref[pl.ds(partner(row, site, j), 1), :]
        out_ref[j, LIST : LIST + 1, :] = wanted.astype(jnp.float32)


def hazard_kernel(levels, own_ref, rup_ref, out_ref, pre_ref, acc_ref):
    blocks = rup_ref.shape[0]
    tiles = out_ref.shape[1] // levels
    units = LANES // SUBLANES
    step = LEVEL_RANGE / (levels - 1)
    wide = lambda i: jnp.broadcast_to(own_ref[i : i + 1, :], (SUBLANES, LANES))
    sigma, shift = wide(3 * tiles), wide(3 * tiles + 1)
    sites = [[wide(i * tiles + t) for i in range(3)] for t in range(tiles)]
    acc_ref[...] = jnp.zeros_like(acc_ref)
    part = lax.broadcasted_iota(jnp.int32, (4 * SUBLANES, 5 * LANES), 0)
    which = lax.broadcasted_iota(jnp.int32, (4 * SUBLANES, 5 * LANES), 1) >> 7
    chosen = (part < 3 * SUBLANES) & ((part & (SUBLANES - 1)) == which)
    spread_out = jnp.where(chosen, 1.0, 0.0).astype(jnp.bfloat16)

    def prepare(b):
        raw = rup_ref[b]
        index = jnp.broadcast_to(raw[4:5], (SUBLANES, LANES)).astype(jnp.int32)
        inverse = 1.0 / (lane_gather(sigma, index)[0:1] * math.sqrt(2.0))
        base = -1.0 + (raw[2:3] - 6.5) + lane_gather(shift, index)[0:1]
        zero = jnp.zeros((3, LANES), jnp.float32)
        rows = jnp.concatenate([raw[0:2], base, inverse, 0.5 * raw[3:4], zero], axis=0)
        thirds = [third.astype(jnp.float32) for third in split_in_three(rows)]
        stack = jnp.concatenate(thirds + [jnp.zeros_like(rows)], axis=0).astype(jnp.bfloat16)
        columns = lax.dot_general(
            stack, spread_out, (((0,), (0,)), ((), ())), preferred_element_type=jnp.float32
        )
        for u in range(units):
            x, y, base, inverse, rate = [
                columns[u * SUBLANES : (u + 1) * SUBLANES, p * LANES : (p + 1) * LANES]
                for p in range(5)
            ]
            k = b * units + u
            pre_ref[0, k] = rate
            pre_ref[1, k] = inverse * step
            for t in range(tiles):
                site_x, site_y, amp = sites[t]
                dx = site_x - x
                dy = site_y - y
                median = base + amp - 0.6 * jnp.log((dx * dx + dy * dy + 100.0) * 0.01)
                pre_ref[2 + t, k] = (LEVEL_FIRST - median) * inverse

    together = 8

    def prepare_some(g, carry):
        for i in range(together):
            prepare(g * together + i)
        return carry

    lax.fori_loop(0, blocks // together, prepare_some, 0)
    unroll = 2 * units

    for t in range(tiles):

        def add(g, carry):
            total = [None] * levels
            for u in range(unroll):
                k = g * unroll + u
                rate = pre_ref[0, k]
                gap = pre_ref[1, k]
                z = pre_ref[2 + t, k]
                whole = rate if u == 0 else whole + rate
                for l in range(levels):
                    term = rate * lax.erf(z)
                    total[l] = term if u == 0 else total[l] + term
                    if l < levels - 1:
                        z = z + gap
            for l in range(levels):
                at = t * levels + l
                acc_ref[at] = acc_ref[at] + (whole - total[l])
            return carry

        lax.fori_loop(0, blocks * units // unroll, add, 0)
    for t in range(tiles):
        for q in range(0, levels, SUBLANES):
            rates = jnp.concatenate(
                [
                    jnp.sum(acc_ref[t * levels + l], axis=0, keepdims=True)
                    for l in range(q, q + SUBLANES)
                ],
                axis=0,
            )
            hazard = 1.0 - jnp.exp(-rates)
            for b in range(blocks):
                out_ref[b, t * levels + q : t * levels + q + SUBLANES, :] = hazard
    for b in range(blocks):
        out_ref[b, tiles * levels : tiles * levels + SUBLANES, :] = jnp.broadcast_to(
            rup_ref[b, LIST : LIST + 1, :], (SUBLANES, LANES)
        )


def pick_by_product(lhs_ref, levels, index):
    span = lhs_ref.shape[1] // 3
    blocks = lhs_ref.shape[0] // levels
    width = index.shape[1]
    low = index & (span - 1)
    high = jnp.broadcast_to(index >> (span.bit_length() - 1), (SUBLANES, width))
    match = lax.broadcasted_iota(jnp.int32, (span, width), 0) == low
    onehot = jnp.where(match, 1.0, 0.0).astype(jnp.bfloat16)
    found = jnp.dot(
        lhs_ref[...],
        jnp.concatenate([onehot] * 3, axis=0),
        preferred_element_type=jnp.float32,
    )
    picked = [jnp.zeros((SUBLANES, width), jnp.float32)] * (levels // SUBLANES)
    for b in range(blocks):
        here = high == b
        for q in range(len(picked)):
            at = b * levels + q * SUBLANES
            picked[q] = jnp.where(here, found[at : at + SUBLANES], picked[q])
    return picked


def relay_kernel(levels, blocks_ref, send_ref, lhs_ref):
    blocks, rows, _ = blocks_ref.shape
    groups = levels // SUBLANES
    tiles = rows // levels
    lists = tiles * levels
    row, site = place()
    span = tiles * LANES
    for b in range(blocks):
        for t in range(tiles):
            thirds = split_in_three(blocks_ref[b, t * levels : (t + 1) * levels, :])
            for i in range(3):
                at = i * span + t * LANES
                lhs_ref[b * levels : (b + 1) * levels, at : at + LANES] = thirds[i]

    def by_product(k):
        index = jnp.concatenate([blocks_ref[k + i, lists : lists + 1, :] for i in range(2)], axis=1)
        picked = pick_by_product(lhs_ref, levels, index.astype(jnp.int32))
        for i in range(2):
            owner = partner(k + i, site, row)
            for q in range(groups):
                send_ref[owner, q * SUBLANES : (q + 1) * SUBLANES, :] = picked[q][
                    :, i * LANES : (i + 1) * LANES
                ]

    def by_gather(k):
        index = blocks_ref[k, lists : lists + SUBLANES, :].astype(jnp.int32)
        lane = index & (LANES - 1)
        tile = index >> 7
        picked = [jnp.zeros((SUBLANES, LANES), jnp.float32)] * groups
        for c in range(blocks * tiles):
            b, t = c // tiles, c % tiles
            here = tile == c
            for q in range(groups):
                at = t * levels + q * SUBLANES
                picked[q] = jnp.where(
                    here, lane_gather(blocks_ref[b, at : at + SUBLANES, :], lane), picked[q]
                )
        owner = partner(k, site, row)
        for q in range(groups):
            send_ref[owner, q * SUBLANES : (q + 1) * SUBLANES, :] = picked[q]

    products = blocks * 5 // 16
    for i in range(products):
        by_product(2 * i)
        by_gather(2 * products + i)
    for k in range(3 * products, blocks):
        by_gather(k)


def table_kernel(source_ref, pick_ref, count_ref, table_ref, slot_ref, split_ref):
    source = source_ref[...]
    count = jnp.zeros(source.shape, jnp.int32)
    for s in range(count_ref.shape[1]):
        count = jnp.where(source == s, count_ref[0, s], count)
    pick = pick_ref[...]
    quotient = jnp.floor(pick.astype(jnp.float32) / count.astype(jnp.float32)).astype(jnp.int32)
    slot = pick - quotient * count
    slot = jnp.where(slot < 0, slot + count, slot)
    slot_ref[...] = jnp.where(slot >= count, slot - count, slot)
    classes = table_ref.shape[1]
    table = table_ref[...]
    high = table.astype(jnp.bfloat16)
    split_ref[:, 0:classes] = high
    split_ref[:, classes : 2 * classes] = (table - high.astype(jnp.float32)).astype(jnp.bfloat16)


def loss_kernel(curves_ref, source_ref, slot_ref, class_ref, split_ref, out_ref, lhs_ref):
    sources, levels, _ = curves_ref.shape
    bins, assets = out_ref.shape
    classes = split_ref.shape[1] // 2
    groups = levels // SUBLANES
    width = 2 * LANES
    for s in range(sources):
        thirds = split_in_three(curves_ref[s])
        for i in range(3):
            at = i * width + (s % 2) * LANES
            lhs_ref[s // 2 * levels : (s // 2 + 1) * levels, at : at + LANES] = thirds[i]
    for t in range(assets // width):
        pair = range(2 * t, 2 * t + 2)
        if t % PRODUCTS == 0:
            index = jnp.concatenate(
                [source_ref[i : i + 1, :] * LANES + slot_ref[i : i + 1, :] for i in pair], axis=1
            )
            picked = pick_by_product(lhs_ref, levels, index)
        else:
            halves = []
            for i in pair:
                lane = jnp.broadcast_to(slot_ref[i : i + 1, :], (SUBLANES, LANES))
                which = jnp.broadcast_to(source_ref[i : i + 1, :], (SUBLANES, LANES))
                half = [jnp.zeros((SUBLANES, LANES), jnp.float32)] * groups
                for s in range(sources):
                    here = which == s
                    for q in range(groups):
                        part = curves_ref[s, q * SUBLANES : (q + 1) * SUBLANES, :]
                        half[q] = jnp.where(here, lane_gather(part, lane), half[q])
                halves.append(half)
            picked = [jnp.concatenate([h[q] for h in halves], axis=1) for q in range(groups)]
        curves = jnp.concatenate(picked, axis=0)
        following = jnp.concatenate([curves[1:], jnp.zeros((1, width), jnp.float32)], axis=0)
        occurrence = curves - following
        kinds = jnp.concatenate([class_ref[i : i + 1, :] for i in pair], axis=1)
        match = lax.broadcasted_iota(jnp.int32, (classes, width), 0) == kinds
        onehot = jnp.where(match, 1.0, 0.0).astype(jnp.bfloat16)
        both = jnp.concatenate([onehot, onehot], axis=0)
        chosen = jnp.dot(split_ref[...], both, preferred_element_type=jnp.float32)
        total = jnp.zeros((bins, width), jnp.float32)
        for l in range(levels):
            total = total + occurrence[l : l + 1, :] * chosen[l * bins : (l + 1) * bins, :]
        out_ref[:, t * width : (t + 1) * width] = total


def per_device(
    site_x,
    site_y,
    site_amp,
    rup_x,
    rup_y,
    rup_mag,
    rup_rate,
    rup_source,
    src_sigma,
    src_shift,
    relay_sites,
    relay_count,
    asset_source,
    asset_pick,
    asset_class,
    vulnerability,
    rows,
    columns,
):
    classes, levels, bins = vulnerability.shape
    sites = site_x.shape[0]
    sources, capacity = relay_sites.shape[2:]
    assets = asset_source.shape[0]
    own_sites = sites // rows
    limit = pltpu.CompilerParams(vmem_limit_bytes=48 * 2**20)

    line = lambda a: a.reshape(1, -1)
    square = lambda a: a.reshape(-1, LANES)
    tiles = own_sites // LANES
    packed, own = pl.pallas_call(
        pack_kernel,
        out_shape=(
            jax.ShapeDtypeStruct((rows, SUBLANES, LANES), jnp.float32),
            jax.ShapeDtypeStruct((3 * tiles + 2, LANES), jnp.float32),
        ),
        in_specs=[VMEM] * 11,
        out_specs=(VMEM, VMEM),
    )(
        line(rup_x),
        line(rup_y),
        line(rup_mag),
        line(rup_rate),
        line(rup_source),
        relay_sites[0, 0],
        line(src_sigma),
        line(src_shift),
        square(site_x),
        square(site_y),
        square(site_amp),
    )
    groups = [[j * columns + partner(0, d, j) for j in range(rows)] for d in range(columns)]
    ruptures = lax.all_to_all(packed, ("rup", "site"), 0, 0, axis_index_groups=groups, tiled=True)
    height = tiles * levels + SUBLANES
    copies = pl.pallas_call(
        functools.partial(hazard_kernel, levels),
        out_shape=jax.ShapeDtypeStruct((rows, height, LANES), jnp.float32),
        in_specs=[VMEM] * 2,
        out_specs=VMEM,
        scratch_shapes=[
            pltpu.VMEM((2 + tiles, rows * LANES // SUBLANES, SUBLANES, LANES), jnp.float32),
            pltpu.VMEM((tiles * levels, SUBLANES, LANES), jnp.float32),
        ],
        compiler_params=limit,
    )(own, ruptures)
    blocks = lax.all_to_all(copies, "rup", 0, 0, tiled=True)
    hazard = blocks[:, : tiles * levels].reshape(rows, tiles, levels, LANES)
    hazard = jnp.transpose(hazard, (2, 0, 1, 3)).reshape(levels, sites)
    send = pl.pallas_call(
        functools.partial(relay_kernel, levels),
        out_shape=jax.ShapeDtypeStruct((columns, levels, capacity), jnp.float32),
        in_specs=[VMEM],
        out_specs=VMEM,
        scratch_shapes=[pltpu.VMEM((rows * levels, 3 * own_sites), jnp.bfloat16)],
        compiler_params=limit,
    )(blocks)
    curves = lax.all_to_all(send, "site", 0, 0, tiled=True)
    table = jnp.transpose(vulnerability, (1, 2, 0)).reshape(levels * bins, classes)
    slot, split = pl.pallas_call(
        table_kernel,
        out_shape=(
            jax.ShapeDtypeStruct((assets // LANES, LANES), jnp.int32),
            jax.ShapeDtypeStruct((levels * bins, 2 * classes), jnp.bfloat16),
        ),
        in_specs=[VMEM, VMEM, SMEM, VMEM],
        out_specs=(VMEM, VMEM),
        compiler_params=limit,
    )(square(asset_source), square(asset_pick), relay_count.reshape(1, sources), table)
    losses = pl.pallas_call(
        loss_kernel,
        out_shape=jax.ShapeDtypeStruct((bins, assets), jnp.float32),
        in_specs=[VMEM] * 5,
        out_specs=VMEM,
        scratch_shapes=[pltpu.VMEM((sources * levels // 2, 6 * LANES), jnp.bfloat16)],
        compiler_params=limit,
    )(curves, square(asset_source), slot, square(asset_class), split)
    return hazard, losses


def solution(mesh):
    return jax.shard_map(
        functools.partial(per_device, rows=mesh.shape["rup"], columns=mesh.shape["site"]),
        mesh=mesh,
        in_specs=(
            P("site"),
            P("site"),
            P("site"),
            P("rup"),
            P("rup"),
            P("rup"),
            P("rup"),
            P("rup"),
            P(),
            P(),
            P("rup", "site", None, None),
            P("rup", "site", None),
            P(("rup", "site")),
            P(("rup", "site")),
            P(("rup", "site")),
            P(),
        ),
        out_specs=(P(None, "site"), P(None, ("rup", "site"))),
        check_vma=False,
    )
```

```python
import functools
import math

import jax
import jax.numpy as jnp
from jax import lax
from jax.experimental import pallas as pl
from jax.experimental.pallas import tpu as pltpu
from jax.sharding import PartitionSpec as P

LANES = 128
SUBLANES = 8
LIST = 5
UNROLL = 24
PRODUCTS = 2
VMEM = pl.BlockSpec(memory_space=pltpu.VMEM)
SMEM = pl.BlockSpec(memory_space=pltpu.SMEM)
LEVEL_FIRST = math.log(0.005)
LEVEL_RANGE = math.log(600.0)


def lane_gather(row, index):
    return jnp.take_along_axis(row, index, axis=1, mode="promise_in_bounds")


def partner(row, site, other):
    inner = lambda r: (((r & 3) + 1) >> 1) & 1
    south = lambda r: 2 * inner(r) - (r >> 2)
    z_lo = (site >> 3) ^ inner(row) ^ inner(other)
    y = (((site >> 1) & 3) - south(row) + south(other)) & 3
    core = (site & 1) ^ ((row & 3) >> 1) ^ ((other & 3) >> 1)
    return z_lo * 8 + y * 2 + core


def place():
    return lax.axis_index("rup"), lax.axis_index("site")


def split_in_three(value):
    high = value.astype(jnp.bfloat16)
    rest = value - high.astype(jnp.float32)
    middle = rest.astype(jnp.bfloat16)
    return high, middle, (rest - middle.astype(jnp.float32)).astype(jnp.bfloat16)


def pack_kernel(x_ref, y_ref, mag_ref, rate_ref, source_ref, relay_ref, out_ref):
    row, site = place()
    source = source_ref[...].astype(jnp.float32)
    zero = jnp.zeros((1, LANES), jnp.float32)
    packed = jnp.concatenate(
        [x_ref[...], y_ref[...], mag_ref[...], rate_ref[...], source, zero, zero, zero], axis=0
    )
    for j in range(out_ref.shape[0]):
        out_ref[j] = packed
        wanted = relay_ref[pl.ds(partner(row, site, j), 1), :]
        out_ref[j, LIST : LIST + 1, :] = wanted.astype(jnp.float32)


def wide(row):
    return jnp.broadcast_to(row, (SUBLANES, LANES))


def spreading():
    part = lax.broadcasted_iota(jnp.int32, (4 * SUBLANES, 5 * LANES), 0)
    which = lax.broadcasted_iota(jnp.int32, (4 * SUBLANES, 5 * LANES), 1) >> 7
    chosen = (part < 3 * SUBLANES) & ((part & (SUBLANES - 1)) == which)
    return jnp.where(chosen, 1.0, 0.0).astype(jnp.bfloat16)


def prepare(raw, at, levels, own_ref, spread_out, pre_ref):
    tiles = pre_ref.shape[0] - 2
    units = LANES // SUBLANES
    step = LEVEL_RANGE / (levels - 1)
    index = wide(raw[4:5]).astype(jnp.int32)
    sigma = wide(own_ref[3 * tiles : 3 * tiles + 1, :])
    shift = wide(own_ref[3 * tiles + 1 : 3 * tiles + 2, :])
    inverse = 1.0 / (lane_gather(sigma, index)[0:1] * math.sqrt(2.0))
    base = -1.0 + (raw[2:3] - 6.5) + lane_gather(shift, index)[0:1]
    zero = jnp.zeros((3, LANES), jnp.float32)
    rows = jnp.concatenate([raw[0:2], base, inverse, 0.5 * raw[3:4], zero], axis=0)
    thirds = [third.astype(jnp.float32) for third in split_in_three(rows)]
    stack = jnp.concatenate(thirds + [jnp.zeros_like(rows)], axis=0).astype(jnp.bfloat16)
    columns = lax.dot_general(
        stack, spread_out, (((0,), (0,)), ((), ())), preferred_element_type=jnp.float32
    )
    sites = [[wide(own_ref[i * tiles + t : i * tiles + t + 1, :]) for i in range(3)] for t in range(tiles)]
    for u in range(units):
        x, y, base, inverse, rate = [
            columns[u * SUBLANES : (u + 1) * SUBLANES, p * LANES : (p + 1) * LANES]
            for p in range(5)
        ]
        k = at * units + u
        pre_ref[0, k] = rate
        pre_ref[1, k] = inverse * step
        for t in range(tiles):
            site_x, site_y, amp = sites[t]
            dx = site_x - x
            dy = site_y - y
            median = base + amp - 0.6 * jnp.log((dx * dx + dy * dy + 100.0) * 0.01)
            pre_ref[2 + t, k] = (LEVEL_FIRST - median) * inverse


def tails(first, count, t, levels, pre_ref):
    total = [None] * levels
    for u in range(count):
        rate = pre_ref[0, first + u]
        gap = pre_ref[1, first + u]
        z = pre_ref[2 + t, first + u]
        whole = rate if u == 0 else whole + rate
        for l in range(levels):
            term = rate * lax.erf(z)
            total[l] = term if u == 0 else total[l] + term
            if l < levels - 1:
                z = z + gap
    return [whole - part for part in total]


def own_kernel(
    levels, rup_ref, sx_ref, sy_ref, amp_ref, sigma_ref, shift_ref, own_ref, acc_ref, pre_ref
):
    rows = rup_ref.shape[0]
    row = place()[0]
    tiles = sx_ref.shape[0] // rows
    for i, ref in enumerate((sx_ref, sy_ref, amp_ref)):
        own_ref[i * tiles : (i + 1) * tiles, :] = ref[pl.ds(row * tiles, tiles), :]
    sources = sigma_ref.shape[1]
    own_ref[3 * tiles : 3 * tiles + 2, :] = jnp.zeros((2, LANES), jnp.float32)
    own_ref[3 * tiles : 3 * tiles + 1, 0:sources] = sigma_ref[...]
    own_ref[3 * tiles + 1 : 3 * tiles + 2, 0:sources] = shift_ref[...]
    prepare(rup_ref[0], 0, levels, own_ref, spreading(), pre_ref)
    for t in range(tiles):
        sums = tails(0, LANES // SUBLANES, t, levels, pre_ref)
        for l in range(levels):
            acc_ref[t * levels + l] = sums[l]


def hazard_kernel(levels, own_ref, sums_ref, rup_ref, out_ref, pre_ref, acc_ref):
    blocks = rup_ref.shape[0]
    tiles = out_ref.shape[1] // levels
    units = LANES // SUBLANES
    row = place()[0]
    spread_out = spreading()
    acc_ref[...] = sums_ref[...]
    others = blocks - 1
    together = 5

    def prepare_some(g, carry):
        for i in range(together):
            at = g * together + i
            block = (row + 1 + at) & (blocks - 1)
            prepare(rup_ref[block], at, levels, own_ref, spread_out, pre_ref)
        return carry

    lax.fori_loop(0, others // together, prepare_some, 0)
    unroll = UNROLL

    for t in range(tiles):

        def add(g, carry):
            sums = tails(g * unroll, unroll, t, levels, pre_ref)
            for l in range(levels):
                at = t * levels + l
                acc_ref[at] = acc_ref[at] + sums[l]
            return carry

        lax.fori_loop(0, others * units // unroll, add, 0)
    for t in range(tiles):
        for q in range(0, levels, SUBLANES):
            rates = jnp.concatenate(
                [
                    jnp.sum(acc_ref[t * levels + l], axis=0, keepdims=True)
                    for l in range(q, q + SUBLANES)
                ],
                axis=0,
            )
            hazard = 1.0 - jnp.exp(-rates)
            for b in range(blocks):
                out_ref[b, t * levels + q : t * levels + q + SUBLANES, :] = hazard
    for b in range(blocks):
        out_ref[b, tiles * levels : tiles * levels + SUBLANES, :] = wide(
            rup_ref[b, LIST : LIST + 1, :]
        )


def pick_by_product(lhs_ref, levels, index):
    span = lhs_ref.shape[1] // 3
    blocks = lhs_ref.shape[0] // levels
    width = index.shape[1]
    low = index & (span - 1)
    high = jnp.broadcast_to(index >> (span.bit_length() - 1), (SUBLANES, width))
    match = lax.broadcasted_iota(jnp.int32, (span, width), 0) == low
    onehot = jnp.where(match, 1.0, 0.0).astype(jnp.bfloat16)
    found = jnp.dot(
        lhs_ref[...],
        jnp.concatenate([onehot] * 3, axis=0),
        preferred_element_type=jnp.float32,
    )
    picked = [jnp.zeros((SUBLANES, width), jnp.float32)] * (levels // SUBLANES)
    for b in range(blocks):
        here = high == b
        for q in range(len(picked)):
            at = b * levels + q * SUBLANES
            picked[q] = jnp.where(here, found[at : at + SUBLANES], picked[q])
    return picked


def relay_kernel(levels, blocks_ref, send_ref, lhs_ref):
    blocks, rows, _ = blocks_ref.shape
    groups = levels // SUBLANES
    tiles = rows // levels
    lists = tiles * levels
    row, site = place()
    span = tiles * LANES
    for b in range(blocks):
        for t in range(tiles):
            thirds = split_in_three(blocks_ref[b, t * levels : (t + 1) * levels, :])
            for i in range(3):
                at = i * span + t * LANES
                lhs_ref[b * levels : (b + 1) * levels, at : at + LANES] = thirds[i]

    def by_product(k):
        index = jnp.concatenate([blocks_ref[k + i, lists : lists + 1, :] for i in range(2)], axis=1)
        picked = pick_by_product(lhs_ref, levels, index.astype(jnp.int32))
        for i in range(2):
            owner = partner(k + i, site, row)
            for q in range(groups):
                send_ref[owner, q * SUBLANES : (q + 1) * SUBLANES, :] = picked[q][
                    :, i * LANES : (i + 1) * LANES
                ]

    def by_gather(k):
        index = blocks_ref[k, lists : lists + SUBLANES, :].astype(jnp.int32)
        lane = index & (LANES - 1)
        tile = index >> 7
        picked = [jnp.zeros((SUBLANES, LANES), jnp.float32)] * groups
        for c in range(blocks * tiles):
            b, t = c // tiles, c % tiles
            here = tile == c
            for q in range(groups):
                at = t * levels + q * SUBLANES
                picked[q] = jnp.where(
                    here, lane_gather(blocks_ref[b, at : at + SUBLANES, :], lane), picked[q]
                )
        owner = partner(k, site, row)
        for q in range(groups):
            send_ref[owner, q * SUBLANES : (q + 1) * SUBLANES, :] = picked[q]

    products = blocks * 5 // 16
    for i in range(products):
        by_product(2 * i)
        by_gather(2 * products + i)
    for k in range(3 * products, blocks):
        by_gather(k)


def table_kernel(source_ref, pick_ref, count_ref, table_ref, slot_ref, split_ref):
    source = source_ref[...]
    count = jnp.zeros(source.shape, jnp.int32)
    for s in range(count_ref.shape[1]):
        count = jnp.where(source == s, count_ref[0, s], count)
    pick = pick_ref[...]
    quotient = jnp.floor(pick.astype(jnp.float32) / count.astype(jnp.float32)).astype(jnp.int32)
    slot = pick - quotient * count
    slot = jnp.where(slot < 0, slot + count, slot)
    slot_ref[...] = jnp.where(slot >= count, slot - count, slot)
    classes = table_ref.shape[1]
    table = table_ref[...]
    high = table.astype(jnp.bfloat16)
    split_ref[:, 0:classes] = high
    split_ref[:, classes : 2 * classes] = (table - high.astype(jnp.float32)).astype(jnp.bfloat16)


def loss_kernel(
    curves_ref, source_ref, slot_ref, class_ref, split_ref, out_ref, lhs_ref, change_ref
):
    sources, levels, _ = curves_ref.shape
    bins, assets = out_ref.shape
    classes = split_ref.shape[1] // 2
    groups = levels // SUBLANES
    width = 2 * LANES
    for s in range(sources):
        thirds = split_in_three(curves_ref[s])
        for i in range(3):
            at = i * width + (s % 2) * LANES
            lhs_ref[s // 2 * levels : (s // 2 + 1) * levels, at : at + LANES] = thirds[i]

    def by_product(t):
        index = jnp.concatenate(
            [source_ref[i : i + 1, :] * LANES + slot_ref[i : i + 1, :] for i in (2 * t, 2 * t + 1)],
            axis=1,
        )
        return pick_by_product(lhs_ref, levels, index)

    def by_gather(t):
        halves = []
        for i in (2 * t, 2 * t + 1):
            lane = wide(slot_ref[i : i + 1, :])
            which = wide(source_ref[i : i + 1, :])
            half = [jnp.zeros((SUBLANES, LANES), jnp.float32)] * groups
            for s in range(sources):
                here = which == s
                for q in range(groups):
                    part = curves_ref[s, q * SUBLANES : (q + 1) * SUBLANES, :]
                    half[q] = jnp.where(here, lane_gather(part, lane), half[q])
            halves.append(half)
        return [jnp.concatenate([h[q] for h in halves], axis=1) for q in range(groups)]

    for t in range(assets // width):
        curves = jnp.concatenate(by_product(t) if t < PRODUCTS else by_gather(t), axis=0)
        following = jnp.concatenate([curves[1:], jnp.zeros((1, width), jnp.float32)], axis=0)
        change_ref[:, t * width : (t + 1) * width] = curves - following
    for t in range(assets // width):
        across = slice(t * width, (t + 1) * width)
        kinds = jnp.concatenate([class_ref[i : i + 1, :] for i in (2 * t, 2 * t + 1)], axis=1)
        match = lax.broadcasted_iota(jnp.int32, (classes, width), 0) == kinds
        onehot = jnp.where(match, 1.0, 0.0).astype(jnp.bfloat16)
        both = jnp.concatenate([onehot, onehot], axis=0)
        chosen = jnp.dot(split_ref[...], both, preferred_element_type=jnp.float32)
        total = jnp.zeros((bins, width), jnp.float32)
        for l in range(levels):
            part = chosen[l * bins : (l + 1) * bins, :]
            total = total + change_ref[l : l + 1, across] * part
        out_ref[:, across] = total


def per_device(
    site_x,
    site_y,
    site_amp,
    rup_x,
    rup_y,
    rup_mag,
    rup_rate,
    rup_source,
    src_sigma,
    src_shift,
    relay_sites,
    relay_count,
    asset_source,
    asset_pick,
    asset_class,
    vulnerability,
    rows,
    columns,
):
    classes, levels, bins = vulnerability.shape
    sites = site_x.shape[0]
    sources, capacity = relay_sites.shape[2:]
    assets = asset_source.shape[0]
    own_sites = sites // rows
    limit = pltpu.CompilerParams(vmem_limit_bytes=48 * 2**20)

    line = lambda a: a.reshape(1, -1)
    square = lambda a: a.reshape(-1, LANES)
    tiles = own_sites // LANES
    packed = pl.pallas_call(
        pack_kernel,
        out_shape=jax.ShapeDtypeStruct((rows, SUBLANES, LANES), jnp.float32),
        in_specs=[VMEM] * 6,
        out_specs=VMEM,
    )(
        line(rup_x),
        line(rup_y),
        line(rup_mag),
        line(rup_rate),
        line(rup_source),
        relay_sites[0, 0],
    )
    units = rows * LANES // SUBLANES
    sums_shape = (tiles * levels, SUBLANES, LANES)
    own, sums = pl.pallas_call(
        functools.partial(own_kernel, levels),
        out_shape=(
            jax.ShapeDtypeStruct((3 * tiles + 2, LANES), jnp.float32),
            jax.ShapeDtypeStruct(sums_shape, jnp.float32),
        ),
        in_specs=[VMEM] * 6,
        out_specs=(VMEM, VMEM),
        scratch_shapes=[pltpu.VMEM((2 + tiles, units // rows, SUBLANES, LANES), jnp.float32)],
        compiler_params=limit,
    )(
        packed,
        square(site_x),
        square(site_y),
        square(site_amp),
        line(src_sigma),
        line(src_shift),
    )
    groups = [[j * columns + partner(0, d, j) for j in range(rows)] for d in range(columns)]
    ruptures = lax.all_to_all(packed, ("rup", "site"), 0, 0, axis_index_groups=groups, tiled=True)
    height = tiles * levels + SUBLANES
    copies = pl.pallas_call(
        functools.partial(hazard_kernel, levels),
        out_shape=jax.ShapeDtypeStruct((rows, height, LANES), jnp.float32),
        in_specs=[VMEM] * 3,
        out_specs=VMEM,
        scratch_shapes=[
            pltpu.VMEM((2 + tiles, units, SUBLANES, LANES), jnp.float32),
            pltpu.VMEM(sums_shape, jnp.float32),
        ],
        compiler_params=limit,
    )(own, sums, ruptures)
    blocks = lax.all_to_all(copies, "rup", 0, 0, tiled=True)
    hazard = blocks[:, : tiles * levels].reshape(rows, tiles, levels, LANES)
    hazard = jnp.transpose(hazard, (2, 0, 1, 3)).reshape(levels, sites)
    send = pl.pallas_call(
        functools.partial(relay_kernel, levels),
        out_shape=jax.ShapeDtypeStruct((columns, levels, capacity), jnp.float32),
        in_specs=[VMEM],
        out_specs=VMEM,
        scratch_shapes=[pltpu.VMEM((rows * levels, 3 * own_sites), jnp.bfloat16)],
        compiler_params=limit,
    )(blocks)
    curves = lax.all_to_all(send, "site", 0, 0, tiled=True)
    table = jnp.transpose(vulnerability, (1, 2, 0)).reshape(levels * bins, classes)
    slot, split = pl.pallas_call(
        table_kernel,
        out_shape=(
            jax.ShapeDtypeStruct((assets // LANES, LANES), jnp.int32),
            jax.ShapeDtypeStruct((levels * bins, 2 * classes), jnp.bfloat16),
        ),
        in_specs=[VMEM, VMEM, SMEM, VMEM],
        out_specs=(VMEM, VMEM),
        compiler_params=limit,
    )(square(asset_source), square(asset_pick), relay_count.reshape(1, sources), table)
    losses = pl.pallas_call(
        loss_kernel,
        out_shape=jax.ShapeDtypeStruct((bins, assets), jnp.float32),
        in_specs=[VMEM] * 5,
        out_specs=VMEM,
        scratch_shapes=[
            pltpu.VMEM((sources * levels // 2, 6 * LANES), jnp.bfloat16),
            pltpu.VMEM((levels, assets), jnp.float32),
        ],
        compiler_params=limit,
    )(curves, square(asset_source), slot, square(asset_class), split)
    return hazard, losses


def solution(mesh):
    return jax.shard_map(
        functools.partial(per_device, rows=mesh.shape["rup"], columns=mesh.shape["site"]),
        mesh=mesh,
        in_specs=(
            P("site"),
            P("site"),
            P("site"),
            P("rup"),
            P("rup"),
            P("rup"),
            P("rup"),
            P("rup"),
            P(),
            P(),
            P("rup", "site", None, None),
            P("rup", "site", None),
            P(("rup", "site")),
            P(("rup", "site")),
            P(("rup", "site")),
            P(),
        ),
        out_specs=(P(None, "site"), P(None, ("rup", "site"))),
        check_vma=False,
    )
```

```python
import functools
import math

import jax
import jax.numpy as jnp
from jax import lax
from jax.experimental import pallas as pl
from jax.experimental.pallas import tpu as pltpu
from jax.sharding import PartitionSpec as P

LANES = 128
SUBLANES = 8
LIST = 5
UNROLL = 24
PRODUCTS = 2
VMEM = pl.BlockSpec(memory_space=pltpu.VMEM)
SMEM = pl.BlockSpec(memory_space=pltpu.SMEM)
LEVEL_FIRST = math.log(0.005)
LEVEL_RANGE = math.log(600.0)


def lane_gather(row, index):
    return jnp.take_along_axis(row, index, axis=1, mode="promise_in_bounds")


def partner(row, site, other):
    inner = lambda r: (((r & 3) + 1) >> 1) & 1
    south = lambda r: 2 * inner(r) - (r >> 2)
    z_lo = (site >> 3) ^ inner(row) ^ inner(other)
    y = (((site >> 1) & 3) - south(row) + south(other)) & 3
    core = (site & 1) ^ ((row & 3) >> 1) ^ ((other & 3) >> 1)
    return z_lo * 8 + y * 2 + core


def place():
    return lax.axis_index("rup"), lax.axis_index("site")


def split_in_three(value):
    high = value.astype(jnp.bfloat16)
    rest = value - high.astype(jnp.float32)
    middle = rest.astype(jnp.bfloat16)
    return high, middle, (rest - middle.astype(jnp.float32)).astype(jnp.bfloat16)


def pack_kernel(x_ref, y_ref, mag_ref, rate_ref, source_ref, relay_ref, out_ref):
    row, site = place()
    source = source_ref[...].astype(jnp.float32)
    zero = jnp.zeros((1, LANES), jnp.float32)
    packed = jnp.concatenate(
        [x_ref[...], y_ref[...], mag_ref[...], rate_ref[...], source, zero, zero, zero], axis=0
    )
    for j in range(out_ref.shape[0]):
        out_ref[j] = packed
        wanted = relay_ref[pl.ds(partner(row, site, j), 1), :]
        out_ref[j, LIST : LIST + 1, :] = wanted.astype(jnp.float32)


def wide(row):
    return jnp.broadcast_to(row, (SUBLANES, LANES))


def spreading():
    part = lax.broadcasted_iota(jnp.int32, (4 * SUBLANES, 5 * LANES), 0)
    which = lax.broadcasted_iota(jnp.int32, (4 * SUBLANES, 5 * LANES), 1) >> 7
    chosen = (part < 3 * SUBLANES) & ((part & (SUBLANES - 1)) == which)
    return jnp.where(chosen, 1.0, 0.0).astype(jnp.bfloat16)


def prepare(raw, at, levels, own_ref, spread_out, pre_ref):
    tiles = pre_ref.shape[0] - 2
    units = LANES // SUBLANES
    step = LEVEL_RANGE / (levels - 1)
    index = wide(raw[4:5]).astype(jnp.int32)
    sigma = wide(own_ref[3 * tiles : 3 * tiles + 1, :])
    shift = wide(own_ref[3 * tiles + 1 : 3 * tiles + 2, :])
    inverse = 1.0 / (lane_gather(sigma, index)[0:1] * math.sqrt(2.0))
    base = -1.0 + (raw[2:3] - 6.5) + lane_gather(shift, index)[0:1]
    zero = jnp.zeros((3, LANES), jnp.float32)
    rows = jnp.concatenate([raw[0:2], base, inverse, 0.5 * raw[3:4], zero], axis=0)
    thirds = [third.astype(jnp.float32) for third in split_in_three(rows)]
    stack = jnp.concatenate(thirds + [jnp.zeros_like(rows)], axis=0).astype(jnp.bfloat16)
    columns = lax.dot_general(
        stack, spread_out, (((0,), (0,)), ((), ())), preferred_element_type=jnp.float32
    )
    sites = [[wide(own_ref[i * tiles + t : i * tiles + t + 1, :]) for i in range(3)] for t in range(tiles)]
    for u in range(units):
        x, y, base, inverse, rate = [
            columns[u * SUBLANES : (u + 1) * SUBLANES, p * LANES : (p + 1) * LANES]
            for p in range(5)
        ]
        k = at * units + u
        pre_ref[0, k] = rate
        pre_ref[1, k] = inverse * step
        for t in range(tiles):
            site_x, site_y, amp = sites[t]
            dx = site_x - x
            dy = site_y - y
            median = base + amp - 0.6 * jnp.log((dx * dx + dy * dy + 100.0) * 0.01)
            pre_ref[2 + t, k] = (LEVEL_FIRST - median) * inverse


def tails(first, count, t, levels, pre_ref):
    total = [None] * levels
    for u in range(count):
        rate = pre_ref[0, first + u]
        gap = pre_ref[1, first + u]
        z = pre_ref[2 + t, first + u]
        whole = rate if u == 0 else whole + rate
        for l in range(levels):
            term = rate * lax.erf(z)
            total[l] = term if u == 0 else total[l] + term
            if l < levels - 1:
                z = z + gap
    return [whole - part for part in total]


def own_kernel(
    levels, rup_ref, sx_ref, sy_ref, amp_ref, sigma_ref, shift_ref, own_ref, acc_ref, pre_ref
):
    rows = rup_ref.shape[0]
    row = place()[0]
    tiles = sx_ref.shape[0] // rows
    for i, ref in enumerate((sx_ref, sy_ref, amp_ref)):
        own_ref[i * tiles : (i + 1) * tiles, :] = ref[pl.ds(row * tiles, tiles), :]
    sources = sigma_ref.shape[1]
    own_ref[3 * tiles : 3 * tiles + 2, :] = jnp.zeros((2, LANES), jnp.float32)
    own_ref[3 * tiles : 3 * tiles + 1, 0:sources] = sigma_ref[...]
    own_ref[3 * tiles + 1 : 3 * tiles + 2, 0:sources] = shift_ref[...]
    prepare(rup_ref[0], 0, levels, own_ref, spreading(), pre_ref)
    for t in range(tiles):
        sums = tails(0, LANES // SUBLANES, t, levels, pre_ref)
        for l in range(levels):
            acc_ref[t * levels + l] = sums[l]


def hazard_kernel(levels, own_ref, sums_ref, rup_ref, *refs):
    out_refs, pre_ref, acc_ref = refs[:-2], refs[-2], refs[-1]
    blocks = rup_ref.shape[0]
    heights = len(out_refs)
    tiles = out_refs[0].shape[0] // levels
    units = LANES // SUBLANES
    row = place()[0]
    spread_out = spreading()
    acc_ref[...] = sums_ref[...]
    others = blocks - 1
    together = 5

    def prepare_some(g, carry):
        for i in range(together):
            at = g * together + i
            block = (row + 1 + at) & (blocks - 1)
            prepare(rup_ref[block], at, levels, own_ref, spread_out, pre_ref)
        return carry

    lax.fori_loop(0, others // together, prepare_some, 0)
    unroll = UNROLL

    for t in range(tiles):

        def add(g, carry):
            sums = tails(g * unroll, unroll, t, levels, pre_ref)
            for l in range(levels):
                at = t * levels + l
                acc_ref[at] = acc_ref[at] + sums[l]
            return carry

        lax.fori_loop(0, others * units // unroll, add, 0)
    for t in range(tiles):
        for q in range(0, levels, SUBLANES):
            rates = jnp.concatenate(
                [
                    jnp.sum(acc_ref[t * levels + l], axis=0, keepdims=True)
                    for l in range(q, q + SUBLANES)
                ],
                axis=0,
            )
            hazard = 1.0 - jnp.exp(-rates)
            for out_ref in out_refs:
                out_ref[t * levels + q : t * levels + q + SUBLANES, :] = hazard
    for k, out_ref in enumerate(out_refs):
        height = (row + k) & (heights - 1)
        lists = [rup_ref[x * heights + height, LIST : LIST + 1, :] for x in range(blocks // heights)]
        lists.append(jnp.zeros((SUBLANES - len(lists), LANES), jnp.float32))
        out_ref[tiles * levels :, :] = jnp.concatenate(lists, axis=0)


def merge_kernel(*refs):
    in_refs, out_ref = refs[:-1], refs[-1]
    heights = len(in_refs)
    length = in_refs[0].shape[0] - SUBLANES
    row = place()[0]
    for x in range(out_ref.shape[0]):
        out_ref[x, heights * length :, :] = jnp.zeros((SUBLANES, LANES), jnp.float32)
        for k, in_ref in enumerate(in_refs):
            height = (row - k) & (heights - 1)
            at = pl.multiple_of(height * length, length)
            out_ref[x, pl.ds(at, length), :] = in_ref[0:length, :]
            out_ref[x, pl.ds(heights * length + height, 1), :] = in_ref[
                length + x : length + x + 1, :
            ]


def pick_by_product(lhs_ref, levels, index):
    span = lhs_ref.shape[1] // 3
    blocks = lhs_ref.shape[0] // levels
    width = index.shape[1]
    low = index & (span - 1)
    high = jnp.broadcast_to(index >> (span.bit_length() - 1), (SUBLANES, width))
    match = lax.broadcasted_iota(jnp.int32, (span, width), 0) == low
    onehot = jnp.where(match, 1.0, 0.0).astype(jnp.bfloat16)
    found = jnp.dot(
        lhs_ref[...],
        jnp.concatenate([onehot] * 3, axis=0),
        preferred_element_type=jnp.float32,
    )
    picked = [jnp.zeros((SUBLANES, width), jnp.float32)] * (levels // SUBLANES)
    for b in range(blocks):
        here = high == b
        for q in range(len(picked)):
            at = b * levels + q * SUBLANES
            picked[q] = jnp.where(here, found[at : at + SUBLANES], picked[q])
    return picked


def relay_kernel(levels, span, blocks_ref, send_ref, lhs_ref):
    parts, rows, _ = blocks_ref.shape
    heights = (rows - SUBLANES) * LANES // (levels * span)
    blocks = parts * heights
    groups = levels // SUBLANES
    tiles = span // LANES
    row, site = place()

    def piece(b, t, first, count):
        at = ((b % heights) * tiles + t) * levels + first
        return blocks_ref[b // heights, at : at + count, :]

    def wanted(k):
        at = heights * tiles * levels + k % heights
        return blocks_ref[k // heights, at : at + 1, :].astype(jnp.int32)

    for b in range(blocks):
        for t in range(tiles):
            thirds = split_in_three(piece(b, t, 0, levels))
            for i in range(3):
                at = i * span + t * LANES
                lhs_ref[b * levels : (b + 1) * levels, at : at + LANES] = thirds[i]

    def by_product(k):
        index = jnp.concatenate([wanted(k + i) for i in range(2)], axis=1)
        picked = pick_by_product(lhs_ref, levels, index)
        for i in range(2):
            owner = partner(k + i, site, row)
            for q in range(groups):
                send_ref[owner, q * SUBLANES : (q + 1) * SUBLANES, :] = picked[q][
                    :, i * LANES : (i + 1) * LANES
                ]

    def by_gather(k):
        index = wide(wanted(k))
        lane = index & (LANES - 1)
        tile = index >> 7
        picked = [jnp.zeros((SUBLANES, LANES), jnp.float32)] * groups
        for c in range(blocks * tiles):
            b, t = c // tiles, c % tiles
            here = tile == c
            for q in range(groups):
                part = piece(b, t, q * SUBLANES, SUBLANES)
                picked[q] = jnp.where(here, lane_gather(part, lane), picked[q])
        owner = partner(k, site, row)
        for q in range(groups):
            send_ref[owner, q * SUBLANES : (q + 1) * SUBLANES, :] = picked[q]

    products = blocks * 5 // 16
    for i in range(products):
        by_product(2 * i)
        by_gather(2 * products + i)
    for k in range(3 * products, blocks):
        by_gather(k)


def table_kernel(source_ref, pick_ref, count_ref, table_ref, slot_ref, split_ref):
    source = source_ref[...]
    count = jnp.zeros(source.shape, jnp.int32)
    for s in range(count_ref.shape[1]):
        count = jnp.where(source == s, count_ref[0, s], count)
    pick = pick_ref[...]
    quotient = jnp.floor(pick.astype(jnp.float32) / count.astype(jnp.float32)).astype(jnp.int32)
    slot = pick - quotient * count
    slot = jnp.where(slot < 0, slot + count, slot)
    slot_ref[...] = jnp.where(slot >= count, slot - count, slot)
    classes = table_ref.shape[1]
    table = table_ref[...]
    high = table.astype(jnp.bfloat16)
    split_ref[:, 0:classes] = high
    split_ref[:, classes : 2 * classes] = (table - high.astype(jnp.float32)).astype(jnp.bfloat16)


def loss_kernel(
    curves_ref, source_ref, slot_ref, class_ref, split_ref, out_ref, lhs_ref, change_ref
):
    sources, levels, _ = curves_ref.shape
    bins, assets = out_ref.shape
    classes = split_ref.shape[1] // 2
    groups = levels // SUBLANES
    width = 2 * LANES
    for s in range(sources):
        thirds = split_in_three(curves_ref[s])
        for i in range(3):
            at = i * width + (s % 2) * LANES
            lhs_ref[s // 2 * levels : (s // 2 + 1) * levels, at : at + LANES] = thirds[i]

    def by_product(t):
        index = jnp.concatenate(
            [source_ref[i : i + 1, :] * LANES + slot_ref[i : i + 1, :] for i in (2 * t, 2 * t + 1)],
            axis=1,
        )
        return pick_by_product(lhs_ref, levels, index)

    def by_gather(t):
        halves = []
        for i in (2 * t, 2 * t + 1):
            lane = wide(slot_ref[i : i + 1, :])
            which = wide(source_ref[i : i + 1, :])
            half = [jnp.zeros((SUBLANES, LANES), jnp.float32)] * groups
            for s in range(sources):
                here = which == s
                for q in range(groups):
                    part = curves_ref[s, q * SUBLANES : (q + 1) * SUBLANES, :]
                    half[q] = jnp.where(here, lane_gather(part, lane), half[q])
            halves.append(half)
        return [jnp.concatenate([h[q] for h in halves], axis=1) for q in range(groups)]

    for t in range(assets // width):
        curves = jnp.concatenate(by_product(t) if t < PRODUCTS else by_gather(t), axis=0)
        following = jnp.concatenate([curves[1:], jnp.zeros((1, width), jnp.float32)], axis=0)
        change_ref[:, t * width : (t + 1) * width] = curves - following
    for t in range(assets // width):
        across = slice(t * width, (t + 1) * width)
        kinds = jnp.concatenate([class_ref[i : i + 1, :] for i in (2 * t, 2 * t + 1)], axis=1)
        match = lax.broadcasted_iota(jnp.int32, (classes, width), 0) == kinds
        onehot = jnp.where(match, 1.0, 0.0).astype(jnp.bfloat16)
        both = jnp.concatenate([onehot, onehot], axis=0)
        chosen = jnp.dot(split_ref[...], both, preferred_element_type=jnp.float32)
        total = jnp.zeros((bins, width), jnp.float32)
        for l in range(levels):
            part = chosen[l * bins : (l + 1) * bins, :]
            total = total + change_ref[l : l + 1, across] * part
        out_ref[:, across] = total


def per_device(
    site_x,
    site_y,
    site_amp,
    rup_x,
    rup_y,
    rup_mag,
    rup_rate,
    rup_source,
    src_sigma,
    src_shift,
    relay_sites,
    relay_count,
    asset_source,
    asset_pick,
    asset_class,
    vulnerability,
    rows,
    columns,
):
    classes, levels, bins = vulnerability.shape
    sites = site_x.shape[0]
    sources, capacity = relay_sites.shape[2:]
    assets = asset_source.shape[0]
    own_sites = sites // rows
    limit = pltpu.CompilerParams(vmem_limit_bytes=48 * 2**20)

    line = lambda a: a.reshape(1, -1)
    square = lambda a: a.reshape(-1, LANES)
    tiles = own_sites // LANES
    packed = pl.pallas_call(
        pack_kernel,
        out_shape=jax.ShapeDtypeStruct((rows, SUBLANES, LANES), jnp.float32),
        in_specs=[VMEM] * 6,
        out_specs=VMEM,
    )(
        line(rup_x),
        line(rup_y),
        line(rup_mag),
        line(rup_rate),
        line(rup_source),
        relay_sites[0, 0],
    )
    units = rows * LANES // SUBLANES
    sums_shape = (tiles * levels, SUBLANES, LANES)
    own, sums = pl.pallas_call(
        functools.partial(own_kernel, levels),
        out_shape=(
            jax.ShapeDtypeStruct((3 * tiles + 2, LANES), jnp.float32),
            jax.ShapeDtypeStruct(sums_shape, jnp.float32),
        ),
        in_specs=[VMEM] * 6,
        out_specs=(VMEM, VMEM),
        scratch_shapes=[pltpu.VMEM((2 + tiles, units // rows, SUBLANES, LANES), jnp.float32)],
        compiler_params=limit,
    )(
        packed,
        square(site_x),
        square(site_y),
        square(site_amp),
        line(src_sigma),
        line(src_shift),
    )
    groups = [[j * columns + partner(0, d, j) for j in range(rows)] for d in range(columns)]
    ruptures = lax.all_to_all(packed, ("rup", "site"), 0, 0, axis_index_groups=groups, tiled=True)
    heights = 4
    length = tiles * levels
    copy = jax.ShapeDtypeStruct((length + SUBLANES, LANES), jnp.float32)
    copies = pl.pallas_call(
        functools.partial(hazard_kernel, levels),
        out_shape=(copy,) * heights,
        in_specs=[VMEM] * 3,
        out_specs=(VMEM,) * heights,
        scratch_shapes=[
            pltpu.VMEM((2 + tiles, units, SUBLANES, LANES), jnp.float32),
            pltpu.VMEM(sums_shape, jnp.float32),
        ],
        compiler_params=limit,
    )(own, sums, ruptures)
    along = lambda k: [(r, r // heights * heights + (r + k) % heights) for r in range(rows)]
    far_first = sorted(range(1, heights), key=lambda k: -min(k, heights - k))
    moved = {k: lax.ppermute(copies[k], "rup", along(k)) for k in far_first}
    east = rows // heights
    merged = pl.pallas_call(
        merge_kernel,
        out_shape=jax.ShapeDtypeStruct((east, heights * length + SUBLANES, LANES), jnp.float32),
        in_specs=[VMEM] * heights,
        out_specs=VMEM,
        compiler_params=limit,
    )(copies[0], *[moved[k] for k in range(1, heights)])
    lines = [
        [(x * heights + height) * columns + d for x in range(east)]
        for height in range(heights)
        for d in range(columns)
    ]
    blocks = lax.all_to_all(merged, ("rup", "site"), 0, 0, axis_index_groups=lines, tiled=True)
    hazard = blocks[:, : heights * length].reshape(rows * tiles, levels, LANES)
    hazard = jnp.transpose(hazard, (1, 0, 2)).reshape(levels, sites)
    send = pl.pallas_call(
        functools.partial(relay_kernel, levels, own_sites),
        out_shape=jax.ShapeDtypeStruct((columns, levels, capacity), jnp.float32),
        in_specs=[VMEM],
        out_specs=VMEM,
        scratch_shapes=[pltpu.VMEM((rows * levels, 3 * own_sites), jnp.bfloat16)],
        compiler_params=limit,
    )(blocks)
    curves = lax.all_to_all(send, "site", 0, 0, tiled=True)
    table = jnp.transpose(vulnerability, (1, 2, 0)).reshape(levels * bins, classes)
    slot, split = pl.pallas_call(
        table_kernel,
        out_shape=(
            jax.ShapeDtypeStruct((assets // LANES, LANES), jnp.int32),
            jax.ShapeDtypeStruct((levels * bins, 2 * classes), jnp.bfloat16),
        ),
        in_specs=[VMEM, VMEM, SMEM, VMEM],
        out_specs=(VMEM, VMEM),
        compiler_params=limit,
    )(square(asset_source), square(asset_pick), relay_count.reshape(1, sources), table)
    losses = pl.pallas_call(
        loss_kernel,
        out_shape=jax.ShapeDtypeStruct((bins, assets), jnp.float32),
        in_specs=[VMEM] * 5,
        out_specs=VMEM,
        scratch_shapes=[
            pltpu.VMEM((sources * levels // 2, 6 * LANES), jnp.bfloat16),
            pltpu.VMEM((levels, assets), jnp.float32),
        ],
        compiler_params=limit,
    )(curves, square(asset_source), slot, square(asset_class), split)
    return hazard, losses


def solution(mesh):
    return jax.shard_map(
        functools.partial(per_device, rows=mesh.shape["rup"], columns=mesh.shape["site"]),
        mesh=mesh,
        in_specs=(
            P("site"),
            P("site"),
            P("site"),
            P("rup"),
            P("rup"),
            P("rup"),
            P("rup"),
            P("rup"),
            P(),
            P(),
            P("rup", "site", None, None),
            P("rup", "site", None),
            P(("rup", "site")),
            P(("rup", "site")),
            P(("rup", "site")),
            P(),
        ),
        out_specs=(P(None, "site"), P(None, ("rup", "site"))),
        check_vma=False,
    )
```

```python
import functools
import math

import jax
import jax.numpy as jnp
from jax import lax
from jax.experimental import pallas as pl
from jax.experimental.pallas import tpu as pltpu
from jax.sharding import PartitionSpec as P

LANES = 128
SUBLANES = 8
LIST = 5
UNROLL = 24
PRODUCTS = 2
VMEM = pl.BlockSpec(memory_space=pltpu.VMEM)
SMEM = pl.BlockSpec(memory_space=pltpu.SMEM)
LEVEL_FIRST = math.log(0.005)
LEVEL_RANGE = math.log(600.0)


def lane_gather(row, index):
    return jnp.take_along_axis(row, index, axis=1, mode="promise_in_bounds")


def partner(row, site, other):
    inner = lambda r: (((r & 3) + 1) >> 1) & 1
    south = lambda r: 2 * inner(r) - (r >> 2)
    z_lo = (site >> 3) ^ inner(row) ^ inner(other)
    y = (((site >> 1) & 3) - south(row) + south(other)) & 3
    core = (site & 1) ^ ((row & 3) >> 1) ^ ((other & 3) >> 1)
    return z_lo * 8 + y * 2 + core


def place():
    return lax.axis_index("rup"), lax.axis_index("site")


def split_in_three(value):
    high = value.astype(jnp.bfloat16)
    rest = value - high.astype(jnp.float32)
    middle = rest.astype(jnp.bfloat16)
    return high, middle, (rest - middle.astype(jnp.float32)).astype(jnp.bfloat16)


def pack_kernel(x_ref, y_ref, mag_ref, rate_ref, source_ref, relay_ref, out_ref):
    row, site = place()
    source = source_ref[...].astype(jnp.float32)
    zero = jnp.zeros((1, LANES), jnp.float32)
    packed = jnp.concatenate(
        [x_ref[...], y_ref[...], mag_ref[...], rate_ref[...], source, zero, zero, zero], axis=0
    )
    for j in range(out_ref.shape[0]):
        out_ref[j] = packed
        wanted = relay_ref[pl.ds(partner(row, site, j), 1), :]
        out_ref[j, LIST : LIST + 1, :] = wanted.astype(jnp.float32)


def wide(row):
    return jnp.broadcast_to(row, (SUBLANES, LANES))


def spreading():
    part = lax.broadcasted_iota(jnp.int32, (4 * SUBLANES, 5 * LANES), 0)
    which = lax.broadcasted_iota(jnp.int32, (4 * SUBLANES, 5 * LANES), 1) >> 7
    chosen = (part < 3 * SUBLANES) & ((part & (SUBLANES - 1)) == which)
    return jnp.where(chosen, 1.0, 0.0).astype(jnp.bfloat16)


def prepare(raw, at, levels, own_ref, spread_out, pre_ref):
    tiles = pre_ref.shape[0] - 2
    units = LANES // SUBLANES
    step = LEVEL_RANGE / (levels - 1)
    index = wide(raw[4:5]).astype(jnp.int32)
    sigma = wide(own_ref[3 * tiles : 3 * tiles + 1, :])
    shift = wide(own_ref[3 * tiles + 1 : 3 * tiles + 2, :])
    inverse = 1.0 / (lane_gather(sigma, index)[0:1] * math.sqrt(2.0))
    base = -1.0 + (raw[2:3] - 6.5) + lane_gather(shift, index)[0:1]
    zero = jnp.zeros((3, LANES), jnp.float32)
    rows = jnp.concatenate([raw[0:2], base, inverse, 0.5 * raw[3:4], zero], axis=0)
    thirds = [third.astype(jnp.float32) for third in split_in_three(rows)]
    stack = jnp.concatenate(thirds + [jnp.zeros_like(rows)], axis=0).astype(jnp.bfloat16)
    columns = lax.dot_general(
        stack, spread_out, (((0,), (0,)), ((), ())), preferred_element_type=jnp.float32
    )
    sites = [[wide(own_ref[i * tiles + t : i * tiles + t + 1, :]) for i in range(3)] for t in range(tiles)]
    for u in range(units):
        x, y, base, inverse, rate = [
            columns[u * SUBLANES : (u + 1) * SUBLANES, p * LANES : (p + 1) * LANES]
            for p in range(5)
        ]
        k = at * units + u
        pre_ref[0, k] = rate
        pre_ref[1, k] = inverse * step
        for t in range(tiles):
            site_x, site_y, amp = sites[t]
            dx = site_x - x
            dy = site_y - y
            median = base + amp - 0.6 * jnp.log((dx * dx + dy * dy + 100.0) * 0.01)
            pre_ref[2 + t, k] = (LEVEL_FIRST - median) * inverse


def tails(first, count, t, levels, pre_ref):
    total = [None] * levels
    for u in range(count):
        rate = pre_ref[0, first + u]
        gap = pre_ref[1, first + u]
        z = pre_ref[2 + t, first + u]
        whole = rate if u == 0 else whole + rate
        for l in range(levels):
            term = rate * lax.erf(z)
            total[l] = term if u == 0 else total[l] + term
            if l < levels - 1:
                z = z + gap
    return [whole - part for part in total]


def own_kernel(
    levels, rup_ref, sx_ref, sy_ref, amp_ref, sigma_ref, shift_ref, own_ref, acc_ref, pre_ref
):
    rows = rup_ref.shape[0]
    row = place()[0]
    tiles = sx_ref.shape[0] // rows
    for i, ref in enumerate((sx_ref, sy_ref, amp_ref)):
        own_ref[i * tiles : (i + 1) * tiles, :] = ref[pl.ds(row * tiles, tiles), :]
    sources = sigma_ref.shape[1]
    own_ref[3 * tiles : 3 * tiles + 2, :] = jnp.zeros((2, LANES), jnp.float32)
    own_ref[3 * tiles : 3 * tiles + 1, 0:sources] = sigma_ref[...]
    own_ref[3 * tiles + 1 : 3 * tiles + 2, 0:sources] = shift_ref[...]
    prepare(rup_ref[0], 0, levels, own_ref, spreading(), pre_ref)
    for t in range(tiles):
        sums = tails(0, LANES // SUBLANES, t, levels, pre_ref)
        for l in range(levels):
            acc_ref[t * levels + l] = sums[l]


def hazard_kernel(levels, own_ref, sums_ref, rup_ref, *refs):
    out_refs, pre_ref, acc_ref = refs[:-2], refs[-2], refs[-1]
    blocks = rup_ref.shape[0]
    heights = len(out_refs)
    tiles = out_refs[0].shape[0] // levels
    units = LANES // SUBLANES
    row = place()[0]
    spread_out = spreading()
    acc_ref[...] = sums_ref[...]
    others = blocks - 1
    together = 5

    def prepare_some(g, carry):
        for i in range(together):
            at = g * together + i
            block = (row + 1 + at) & (blocks - 1)
            prepare(rup_ref[block], at, levels, own_ref, spread_out, pre_ref)
        return carry

    lax.fori_loop(0, others // together, prepare_some, 0)
    unroll = UNROLL

    for t in range(tiles):

        def add(g, carry):
            sums = tails(g * unroll, unroll, t, levels, pre_ref)
            for l in range(levels):
                at = t * levels + l
                acc_ref[at] = acc_ref[at] + sums[l]
            return carry

        lax.fori_loop(0, others * units // unroll, add, 0)
    for t in range(tiles):
        for q in range(0, levels, SUBLANES):
            rates = jnp.concatenate(
                [
                    jnp.sum(acc_ref[t * levels + l], axis=0, keepdims=True)
                    for l in range(q, q + SUBLANES)
                ],
                axis=0,
            )
            hazard = 1.0 - jnp.exp(-rates)
            for out_ref in out_refs:
                out_ref[t * levels + q : t * levels + q + SUBLANES, :] = hazard
    for k, out_ref in enumerate(out_refs):
        height = (row & (heights - 1)) ^ k
        lists = [rup_ref[x * heights + height, LIST : LIST + 1, :] for x in range(blocks // heights)]
        lists.append(jnp.zeros((SUBLANES - len(lists), LANES), jnp.float32))
        out_ref[tiles * levels :, :] = jnp.concatenate(lists, axis=0)


def merge_kernel(heights, *refs):
    in_refs, out_refs = refs[:heights], refs[heights:]
    length = in_refs[0].shape[0] - SUBLANES
    row = place()[0]
    for k, out_ref in enumerate(out_refs):
        x = ((row >> 2) + k) & (len(out_refs) - 1)
        out_ref[heights * length :, :] = jnp.zeros((SUBLANES, LANES), jnp.float32)
        for flip, in_ref in enumerate(in_refs):
            height = (row & (heights - 1)) ^ flip
            at = pl.multiple_of(height * length, length)
            out_ref[pl.ds(at, length), :] = in_ref[0:length, :]
            out_ref[pl.ds(heights * length + height, 1), :] = in_ref[pl.ds(length + x, 1), :]


def output_kernel(levels, *refs):
    in_refs, out_ref = refs[:-1], refs[-1]
    row = place()[0]
    tiles = out_ref.shape[1] // (len(in_refs) * LANES)
    for k, in_ref in enumerate(in_refs):
        x = ((row >> 2) - k) & (len(in_refs) - 1)
        for t in range(tiles):
            at = pl.multiple_of((x * tiles + t) * LANES, LANES)
            out_ref[:, pl.ds(at, LANES)] = in_ref[t * levels : (t + 1) * levels, :]


def pick_by_product(lhs_ref, levels, index):
    span = lhs_ref.shape[1] // 3
    blocks = lhs_ref.shape[0] // levels
    width = index.shape[1]
    low = index & (span - 1)
    high = jnp.broadcast_to(index >> (span.bit_length() - 1), (SUBLANES, width))
    match = lax.broadcasted_iota(jnp.int32, (span, width), 0) == low
    onehot = jnp.where(match, 1.0, 0.0).astype(jnp.bfloat16)
    found = jnp.dot(
        lhs_ref[...],
        jnp.concatenate([onehot] * 3, axis=0),
        preferred_element_type=jnp.float32,
    )
    picked = [jnp.zeros((SUBLANES, width), jnp.float32)] * (levels // SUBLANES)
    for b in range(blocks):
        here = high == b
        for q in range(len(picked)):
            at = b * levels + q * SUBLANES
            picked[q] = jnp.where(here, found[at : at + SUBLANES], picked[q])
    return picked


def relay_kernel(levels, span, *refs):
    part_refs, send_ref, lhs_ref = refs[:-2], refs[-2], refs[-1]
    parts = len(part_refs)
    heights = (part_refs[0].shape[0] - SUBLANES) * LANES // (levels * span)
    blocks = parts * heights
    groups = levels // SUBLANES
    tiles = span // LANES
    row, site = place()

    def origin(b):
        return (((row >> 2) - b // heights) & (parts - 1)) * heights + b % heights

    def piece(b, t, first, count):
        at = (b % heights * tiles + t) * levels + first
        return part_refs[b // heights][at : at + count, :]

    def wanted(k):
        at = heights * tiles * levels + k % heights
        return part_refs[k // heights][at : at + 1, :].astype(jnp.int32)

    for b in range(blocks):
        for t in range(tiles):
            thirds = split_in_three(piece(b, t, 0, levels))
            for i in range(3):
                at = i * span + t * LANES
                first = pl.multiple_of(origin(b) * levels, levels)
                lhs_ref[pl.ds(first, levels), at : at + LANES] = thirds[i]

    def by_product(k):
        index = jnp.concatenate([wanted(k + i) for i in range(2)], axis=1)
        picked = pick_by_product(lhs_ref, levels, index)
        for i in range(2):
            owner = partner(origin(k + i), site, row)
            for q in range(groups):
                send_ref[owner, q * SUBLANES : (q + 1) * SUBLANES, :] = picked[q][
                    :, i * LANES : (i + 1) * LANES
                ]

    def by_gather(k):
        index = wide(wanted(k))
        lane = index & (LANES - 1)
        tile = index >> 7
        picked = [jnp.zeros((SUBLANES, LANES), jnp.float32)] * groups
        for c in range(blocks * tiles):
            b, t = c // tiles, c % tiles
            here = tile == origin(b) * tiles + t
            for q in range(groups):
                part = piece(b, t, q * SUBLANES, SUBLANES)
                picked[q] = jnp.where(here, lane_gather(part, lane), picked[q])
        owner = partner(origin(k), site, row)
        for q in range(groups):
            send_ref[owner, q * SUBLANES : (q + 1) * SUBLANES, :] = picked[q]

    products = blocks * 5 // 16
    for i in range(products):
        by_product(2 * i)
        by_gather(2 * products + i)
    for k in range(3 * products, blocks):
        by_gather(k)


def table_kernel(source_ref, pick_ref, count_ref, table_ref, slot_ref, split_ref):
    source = source_ref[...]
    count = jnp.zeros(source.shape, jnp.int32)
    for s in range(count_ref.shape[1]):
        count = jnp.where(source == s, count_ref[0, s], count)
    pick = pick_ref[...]
    quotient = jnp.floor(pick.astype(jnp.float32) / count.astype(jnp.float32)).astype(jnp.int32)
    slot = pick - quotient * count
    slot = jnp.where(slot < 0, slot + count, slot)
    slot_ref[...] = jnp.where(slot >= count, slot - count, slot)
    classes = table_ref.shape[1]
    table = table_ref[...]
    high = table.astype(jnp.bfloat16)
    split_ref[:, 0:classes] = high
    split_ref[:, classes : 2 * classes] = (table - high.astype(jnp.float32)).astype(jnp.bfloat16)


def loss_kernel(
    curves_ref, source_ref, slot_ref, class_ref, split_ref, out_ref, lhs_ref, change_ref
):
    sources, levels, _ = curves_ref.shape
    bins, assets = out_ref.shape
    classes = split_ref.shape[1] // 2
    groups = levels // SUBLANES
    width = 2 * LANES
    for s in range(sources):
        thirds = split_in_three(curves_ref[s])
        for i in range(3):
            at = i * width + (s % 2) * LANES
            lhs_ref[s // 2 * levels : (s // 2 + 1) * levels, at : at + LANES] = thirds[i]

    def by_product(t):
        index = jnp.concatenate(
            [source_ref[i : i + 1, :] * LANES + slot_ref[i : i + 1, :] for i in (2 * t, 2 * t + 1)],
            axis=1,
        )
        return pick_by_product(lhs_ref, levels, index)

    def by_gather(t):
        halves = []
        for i in (2 * t, 2 * t + 1):
            lane = wide(slot_ref[i : i + 1, :])
            which = wide(source_ref[i : i + 1, :])
            half = [jnp.zeros((SUBLANES, LANES), jnp.float32)] * groups
            for s in range(sources):
                here = which == s
                for q in range(groups):
                    part = curves_ref[s, q * SUBLANES : (q + 1) * SUBLANES, :]
                    half[q] = jnp.where(here, lane_gather(part, lane), half[q])
            halves.append(half)
        return [jnp.concatenate([h[q] for h in halves], axis=1) for q in range(groups)]

    for t in range(assets // width):
        curves = jnp.concatenate(by_product(t) if t < PRODUCTS else by_gather(t), axis=0)
        following = jnp.concatenate([curves[1:], jnp.zeros((1, width), jnp.float32)], axis=0)
        change_ref[:, t * width : (t + 1) * width] = curves - following
    for t in range(assets // width):
        across = slice(t * width, (t + 1) * width)
        kinds = jnp.concatenate([class_ref[i : i + 1, :] for i in (2 * t, 2 * t + 1)], axis=1)
        match = lax.broadcasted_iota(jnp.int32, (classes, width), 0) == kinds
        onehot = jnp.where(match, 1.0, 0.0).astype(jnp.bfloat16)
        both = jnp.concatenate([onehot, onehot], axis=0)
        chosen = jnp.dot(split_ref[...], both, preferred_element_type=jnp.float32)
        total = jnp.zeros((bins, width), jnp.float32)
        for l in range(levels):
            part = chosen[l * bins : (l + 1) * bins, :]
            total = total + change_ref[l : l + 1, across] * part
        out_ref[:, across] = total


def per_device(
    site_x,
    site_y,
    site_amp,
    rup_x,
    rup_y,
    rup_mag,
    rup_rate,
    rup_source,
    src_sigma,
    src_shift,
    relay_sites,
    relay_count,
    asset_source,
    asset_pick,
    asset_class,
    vulnerability,
    rows,
    columns,
):
    classes, levels, bins = vulnerability.shape
    sites = site_x.shape[0]
    sources, capacity = relay_sites.shape[2:]
    assets = asset_source.shape[0]
    own_sites = sites // rows
    limit = pltpu.CompilerParams(vmem_limit_bytes=48 * 2**20)

    line = lambda a: a.reshape(1, -1)
    square = lambda a: a.reshape(-1, LANES)
    tiles = own_sites // LANES
    packed = pl.pallas_call(
        pack_kernel,
        out_shape=jax.ShapeDtypeStruct((rows, SUBLANES, LANES), jnp.float32),
        in_specs=[VMEM] * 6,
        out_specs=VMEM,
    )(
        line(rup_x),
        line(rup_y),
        line(rup_mag),
        line(rup_rate),
        line(rup_source),
        relay_sites[0, 0],
    )
    units = rows * LANES // SUBLANES
    sums_shape = (tiles * levels, SUBLANES, LANES)
    own, sums = pl.pallas_call(
        functools.partial(own_kernel, levels),
        out_shape=(
            jax.ShapeDtypeStruct((3 * tiles + 2, LANES), jnp.float32),
            jax.ShapeDtypeStruct(sums_shape, jnp.float32),
        ),
        in_specs=[VMEM] * 6,
        out_specs=(VMEM, VMEM),
        scratch_shapes=[pltpu.VMEM((2 + tiles, units // rows, SUBLANES, LANES), jnp.float32)],
        compiler_params=limit,
    )(
        packed,
        square(site_x),
        square(site_y),
        square(site_amp),
        line(src_sigma),
        line(src_shift),
    )
    groups = [[j * columns + partner(0, d, j) for j in range(rows)] for d in range(columns)]
    ruptures = lax.all_to_all(packed, ("rup", "site"), 0, 0, axis_index_groups=groups, tiled=True)
    heights = 4
    length = tiles * levels
    copy = jax.ShapeDtypeStruct((length + SUBLANES, LANES), jnp.float32)
    copies = pl.pallas_call(
        functools.partial(hazard_kernel, levels),
        out_shape=(copy,) * heights,
        in_specs=[VMEM] * 3,
        out_specs=(VMEM,) * heights,
        scratch_shapes=[
            pltpu.VMEM((2 + tiles, units, SUBLANES, LANES), jnp.float32),
            pltpu.VMEM(sums_shape, jnp.float32),
        ],
        compiler_params=limit,
    )(own, sums, ruptures)
    swap = lambda k: lax.ppermute(copies[k], "rup", [(r, r ^ k) for r in range(rows)])
    east = rows // heights
    merged = pl.pallas_call(
        functools.partial(merge_kernel, heights),
        out_shape=(jax.ShapeDtypeStruct((heights * length + SUBLANES, LANES), jnp.float32),) * east,
        in_specs=[VMEM] * heights,
        out_specs=(VMEM,) * east,
        compiler_params=limit,
    )(copies[0], *[swap(k) for k in range(1, heights)])
    shift = lambda k: lax.ppermute(
        merged[k], "rup", [(r, (r + k * heights) % rows) for r in range(rows)]
    )
    parts = [merged[0]] + [shift(k) for k in range(1, east)]
    hazard = pl.pallas_call(
        functools.partial(output_kernel, levels),
        out_shape=jax.ShapeDtypeStruct((levels, sites), jnp.float32),
        in_specs=[VMEM] * east,
        out_specs=VMEM,
        compiler_params=limit,
    )(*parts)
    send = pl.pallas_call(
        functools.partial(relay_kernel, levels, own_sites),
        out_shape=jax.ShapeDtypeStruct((columns, levels, capacity), jnp.float32),
        in_specs=[VMEM] * east,
        out_specs=VMEM,
        scratch_shapes=[pltpu.VMEM((rows * levels, 3 * own_sites), jnp.bfloat16)],
        compiler_params=limit,
    )(*parts)
    curves = lax.all_to_all(send, "site", 0, 0, tiled=True)
    table = jnp.transpose(vulnerability, (1, 2, 0)).reshape(levels * bins, classes)
    slot, split = pl.pallas_call(
        table_kernel,
        out_shape=(
            jax.ShapeDtypeStruct((assets // LANES, LANES), jnp.int32),
            jax.ShapeDtypeStruct((levels * bins, 2 * classes), jnp.bfloat16),
        ),
        in_specs=[VMEM, VMEM, SMEM, VMEM],
        out_specs=(VMEM, VMEM),
        compiler_params=limit,
    )(square(asset_source), square(asset_pick), relay_count.reshape(1, sources), table)
    losses = pl.pallas_call(
        loss_kernel,
        out_shape=jax.ShapeDtypeStruct((bins, assets), jnp.float32),
        in_specs=[VMEM] * 5,
        out_specs=VMEM,
        scratch_shapes=[
            pltpu.VMEM((sources * levels // 2, 6 * LANES), jnp.bfloat16),
            pltpu.VMEM((levels, assets), jnp.float32),
        ],
        compiler_params=limit,
    )(curves, square(asset_source), slot, square(asset_class), split)
    return hazard, losses


def solution(mesh):
    return jax.shard_map(
        functools.partial(per_device, rows=mesh.shape["rup"], columns=mesh.shape["site"]),
        mesh=mesh,
        in_specs=(
            P("site"),
            P("site"),
            P("site"),
            P("rup"),
            P("rup"),
            P("rup"),
            P("rup"),
            P("rup"),
            P(),
            P(),
            P("rup", "site", None, None),
            P("rup", "site", None),
            P(("rup", "site")),
            P(("rup", "site")),
            P(("rup", "site")),
            P(),
        ),
        out_specs=(P(None, "site"), P(None, ("rup", "site"))),
        check_vma=False,
    )
```

```python
import functools
import math

import jax
import jax.numpy as jnp
from jax import lax
from jax.experimental import pallas as pl
from jax.experimental.pallas import tpu as pltpu
from jax.sharding import PartitionSpec as P

LANES = 128
SUBLANES = 8
LIST = 5
UNROLL = 24
PRODUCTS = 2
VMEM = pl.BlockSpec(memory_space=pltpu.VMEM)
SMEM = pl.BlockSpec(memory_space=pltpu.SMEM)
LEVEL_FIRST = math.log(0.005)
LEVEL_RANGE = math.log(600.0)


def lane_gather(row, index):
    return jnp.take_along_axis(row, index, axis=1, mode="promise_in_bounds")


def partner(row, site, other):
    inner = lambda r: (((r & 3) + 1) >> 1) & 1
    south = lambda r: 2 * inner(r) - (r >> 2)
    z_lo = (site >> 3) ^ inner(row) ^ inner(other)
    y = (((site >> 1) & 3) - south(row) + south(other)) & 3
    core = (site & 1) ^ ((row & 3) >> 1) ^ ((other & 3) >> 1)
    return z_lo * 8 + y * 2 + core


def place():
    return lax.axis_index("rup"), lax.axis_index("site")


def split_in_three(value):
    high = value.astype(jnp.bfloat16)
    rest = value - high.astype(jnp.float32)
    middle = rest.astype(jnp.bfloat16)
    return high, middle, (rest - middle.astype(jnp.float32)).astype(jnp.bfloat16)


def pack_kernel(x_ref, y_ref, mag_ref, rate_ref, source_ref, relay_ref, out_ref):
    row, site = place()
    source = source_ref[...].astype(jnp.float32)
    zero = jnp.zeros((1, LANES), jnp.float32)
    packed = jnp.concatenate(
        [x_ref[...], y_ref[...], mag_ref[...], rate_ref[...], source, zero, zero, zero], axis=0
    )
    for j in range(out_ref.shape[0]):
        out_ref[j] = packed
        wanted = relay_ref[pl.ds(partner(row, site, j), 1), :]
        out_ref[j, LIST : LIST + 1, :] = wanted.astype(jnp.float32)


def wide(row):
    return jnp.broadcast_to(row, (SUBLANES, LANES))


def spreading():
    part = lax.broadcasted_iota(jnp.int32, (4 * SUBLANES, 5 * LANES), 0)
    which = lax.broadcasted_iota(jnp.int32, (4 * SUBLANES, 5 * LANES), 1) >> 7
    chosen = (part < 3 * SUBLANES) & ((part & (SUBLANES - 1)) == which)
    return jnp.where(chosen, 1.0, 0.0).astype(jnp.bfloat16)


def prepare(raw, at, levels, own_ref, spread_out, pre_ref):
    tiles = pre_ref.shape[0] - 2
    units = LANES // SUBLANES
    step = LEVEL_RANGE / (levels - 1)
    index = wide(raw[4:5]).astype(jnp.int32)
    sigma = wide(own_ref[3 * tiles : 3 * tiles + 1, :])
    shift = wide(own_ref[3 * tiles + 1 : 3 * tiles + 2, :])
    inverse = 1.0 / (lane_gather(sigma, index)[0:1] * math.sqrt(2.0))
    base = -1.0 + (raw[2:3] - 6.5) + lane_gather(shift, index)[0:1]
    zero = jnp.zeros((3, LANES), jnp.float32)
    rows = jnp.concatenate([raw[0:2], base, inverse, 0.5 * raw[3:4], zero], axis=0)
    thirds = [third.astype(jnp.float32) for third in split_in_three(rows)]
    stack = jnp.concatenate(thirds + [jnp.zeros_like(rows)], axis=0).astype(jnp.bfloat16)
    columns = lax.dot_general(
        stack, spread_out, (((0,), (0,)), ((), ())), preferred_element_type=jnp.float32
    )
    sites = [[wide(own_ref[i * tiles + t : i * tiles + t + 1, :]) for i in range(3)] for t in range(tiles)]
    for u in range(units):
        x, y, base, inverse, rate = [
            columns[u * SUBLANES : (u + 1) * SUBLANES, p * LANES : (p + 1) * LANES]
            for p in range(5)
        ]
        k = at * units + u
        pre_ref[0, k] = rate
        pre_ref[1, k] = inverse * step
        for t in range(tiles):
            site_x, site_y, amp = sites[t]
            dx = site_x - x
            dy = site_y - y
            median = base + amp - 0.6 * jnp.log((dx * dx + dy * dy + 100.0) * 0.01)
            pre_ref[2 + t, k] = (LEVEL_FIRST - median) * inverse


def tails(first, count, t, levels, pre_ref):
    total = [None] * levels
    for u in range(count):
        rate = pre_ref[0, first + u]
        gap = pre_ref[1, first + u]
        start = pre_ref[2 + t, first + u]
        whole = rate if u == 0 else whole + rate
        for l in range(levels):
            z = z + gap if l % 16 else start + gap * float(l)
            term = rate * lax.erf(z)
            total[l] = term if u == 0 else total[l] + term
    return [whole - part for part in total]


def own_kernel(
    levels, rup_ref, sx_ref, sy_ref, amp_ref, sigma_ref, shift_ref, own_ref, acc_ref, pre_ref
):
    rows = rup_ref.shape[0]
    row = place()[0]
    tiles = sx_ref.shape[0] // rows
    for i, ref in enumerate((sx_ref, sy_ref, amp_ref)):
        own_ref[i * tiles : (i + 1) * tiles, :] = ref[pl.ds(row * tiles, tiles), :]
    sources = sigma_ref.shape[1]
    own_ref[3 * tiles : 3 * tiles + 2, :] = jnp.zeros((2, LANES), jnp.float32)
    own_ref[3 * tiles : 3 * tiles + 1, 0:sources] = sigma_ref[...]
    own_ref[3 * tiles + 1 : 3 * tiles + 2, 0:sources] = shift_ref[...]
    prepare(rup_ref[0], 0, levels, own_ref, spreading(), pre_ref)
    for t in range(tiles):
        sums = tails(0, LANES // SUBLANES, t, levels, pre_ref)
        for l in range(levels):
            acc_ref[t * levels + l] = sums[l]


def hazard_kernel(levels, own_ref, sums_ref, rup_ref, *refs):
    out_refs, pre_ref, acc_ref = refs[:-2], refs[-2], refs[-1]
    blocks = rup_ref.shape[0]
    heights = len(out_refs)
    tiles = out_refs[0].shape[0] // levels
    units = LANES // SUBLANES
    row = place()[0]
    spread_out = spreading()
    acc_ref[...] = sums_ref[...]
    others = blocks - 1
    together = 5

    def prepare_some(g, carry):
        for i in range(together):
            at = g * together + i
            block = (row + 1 + at) & (blocks - 1)
            prepare(rup_ref[block], at, levels, own_ref, spread_out, pre_ref)
        return carry

    lax.fori_loop(0, others // together, prepare_some, 0)
    unroll = UNROLL

    for t in range(tiles):

        def add(g, carry):
            sums = tails(g * unroll, unroll, t, levels, pre_ref)
            for l in range(levels):
                at = t * levels + l
                acc_ref[at] = acc_ref[at] + sums[l]
            return carry

        lax.fori_loop(0, others * units // unroll, add, 0)
    for t in range(tiles):
        for q in range(0, levels, SUBLANES):
            rates = jnp.concatenate(
                [
                    jnp.sum(acc_ref[t * levels + l], axis=0, keepdims=True)
                    for l in range(q, q + SUBLANES)
                ],
                axis=0,
            )
            hazard = 1.0 - jnp.exp(-rates)
            for out_ref in out_refs:
                out_ref[t * levels + q : t * levels + q + SUBLANES, :] = hazard
    for k, out_ref in enumerate(out_refs):
        height = (row & (heights - 1)) ^ k
        lists = [rup_ref[x * heights + height, LIST : LIST + 1, :] for x in range(blocks // heights)]
        lists.append(jnp.zeros((SUBLANES - len(lists), LANES), jnp.float32))
        out_ref[tiles * levels :, :] = jnp.concatenate(lists, axis=0)


def merge_kernel(heights, *refs):
    in_refs, out_refs = refs[:heights], refs[heights:]
    length = in_refs[0].shape[0] - SUBLANES
    row = place()[0]
    for k, out_ref in enumerate(out_refs):
        x = (row >> 2) ^ k
        out_ref[heights * length :, :] = jnp.zeros((SUBLANES, LANES), jnp.float32)
        for flip, in_ref in enumerate(in_refs):
            height = (row & (heights - 1)) ^ flip
            at = pl.multiple_of(height * length, length)
            out_ref[pl.ds(at, length), :] = in_ref[0:length, :]
            out_ref[pl.ds(heights * length + height, 1), :] = in_ref[pl.ds(length + x, 1), :]


def output_kernel(levels, *refs):
    in_refs, out_ref = refs[:-1], refs[-1]
    row = place()[0]
    tiles = out_ref.shape[1] // (len(in_refs) * LANES)
    for k, in_ref in enumerate(in_refs):
        x = (row >> 2) ^ k
        for t in range(tiles):
            at = pl.multiple_of((x * tiles + t) * LANES, LANES)
            out_ref[:, pl.ds(at, LANES)] = in_ref[t * levels : (t + 1) * levels, :]


def pick_by_product(lhs_ref, levels, index):
    span = lhs_ref.shape[1] // 3
    blocks = lhs_ref.shape[0] // levels
    width = index.shape[1]
    low = index & (span - 1)
    high = jnp.broadcast_to(index >> (span.bit_length() - 1), (SUBLANES, width))
    match = lax.broadcasted_iota(jnp.int32, (span, width), 0) == low
    onehot = jnp.where(match, 1.0, 0.0).astype(jnp.bfloat16)
    found = jnp.dot(
        lhs_ref[...],
        jnp.concatenate([onehot] * 3, axis=0),
        preferred_element_type=jnp.float32,
    )
    picked = [jnp.zeros((SUBLANES, width), jnp.float32)] * (levels // SUBLANES)
    for b in range(blocks):
        here = high == b
        for q in range(len(picked)):
            at = b * levels + q * SUBLANES
            picked[q] = jnp.where(here, found[at : at + SUBLANES], picked[q])
    return picked


def relay_kernel(levels, span, *refs):
    part_refs, send_ref, lhs_ref = refs[:-2], refs[-2], refs[-1]
    parts = len(part_refs)
    heights = (part_refs[0].shape[0] - SUBLANES) * LANES // (levels * span)
    blocks = parts * heights
    groups = levels // SUBLANES
    tiles = span // LANES
    row, site = place()

    def origin(b):
        return ((row >> 2) ^ (b // heights)) * heights + b % heights

    def piece(b, t, first, count):
        at = (b % heights * tiles + t) * levels + first
        return part_refs[b // heights][at : at + count, :]

    def wanted(k):
        at = heights * tiles * levels + k % heights
        return part_refs[k // heights][at : at + 1, :].astype(jnp.int32)

    for b in range(blocks):
        for t in range(tiles):
            thirds = split_in_three(piece(b, t, 0, levels))
            for i in range(3):
                at = i * span + t * LANES
                first = pl.multiple_of(origin(b) * levels, levels)
                lhs_ref[pl.ds(first, levels), at : at + LANES] = thirds[i]

    def by_product(k):
        index = jnp.concatenate([wanted(k + i) for i in range(2)], axis=1)
        picked = pick_by_product(lhs_ref, levels, index)
        for i in range(2):
            owner = partner(origin(k + i), site, row)
            for q in range(groups):
                send_ref[owner, q * SUBLANES : (q + 1) * SUBLANES, :] = picked[q][
                    :, i * LANES : (i + 1) * LANES
                ]

    def by_gather(k):
        index = wide(wanted(k))
        lane = index & (LANES - 1)
        tile = index >> 7
        picked = [jnp.zeros((SUBLANES, LANES), jnp.float32)] * groups
        for c in range(blocks * tiles):
            b, t = c // tiles, c % tiles
            here = tile == origin(b) * tiles + t
            for q in range(groups):
                part = piece(b, t, q * SUBLANES, SUBLANES)
                picked[q] = jnp.where(here, lane_gather(part, lane), picked[q])
        owner = partner(origin(k), site, row)
        for q in range(groups):
            send_ref[owner, q * SUBLANES : (q + 1) * SUBLANES, :] = picked[q]

    products = blocks * 5 // 16
    for i in range(products):
        by_product(2 * i)
        by_gather(2 * products + i)
    for k in range(3 * products, blocks):
        by_gather(k)


def table_kernel(source_ref, pick_ref, count_ref, table_ref, slot_ref, split_ref):
    source = source_ref[...]
    count = jnp.zeros(source.shape, jnp.int32)
    for s in range(count_ref.shape[1]):
        count = jnp.where(source == s, count_ref[0, s], count)
    pick = pick_ref[...]
    quotient = jnp.floor(pick.astype(jnp.float32) / count.astype(jnp.float32)).astype(jnp.int32)
    slot = pick - quotient * count
    slot = jnp.where(slot < 0, slot + count, slot)
    slot_ref[...] = jnp.where(slot >= count, slot - count, slot)
    classes = table_ref.shape[1]
    table = table_ref[...]
    high = table.astype(jnp.bfloat16)
    split_ref[:, 0:classes] = high
    split_ref[:, classes : 2 * classes] = (table - high.astype(jnp.float32)).astype(jnp.bfloat16)


def loss_kernel(
    curves_ref, source_ref, slot_ref, class_ref, split_ref, out_ref, lhs_ref, change_ref
):
    sources, levels, _ = curves_ref.shape
    bins, assets = out_ref.shape
    classes = split_ref.shape[1] // 2
    groups = levels // SUBLANES
    width = 2 * LANES
    for s in range(sources):
        thirds = split_in_three(curves_ref[s])
        for i in range(3):
            at = i * width + (s % 2) * LANES
            lhs_ref[s // 2 * levels : (s // 2 + 1) * levels, at : at + LANES] = thirds[i]

    def by_product(t):
        index = jnp.concatenate(
            [source_ref[i : i + 1, :] * LANES + slot_ref[i : i + 1, :] for i in (2 * t, 2 * t + 1)],
            axis=1,
        )
        return pick_by_product(lhs_ref, levels, index)

    def by_gather(t):
        halves = []
        for i in (2 * t, 2 * t + 1):
            lane = wide(slot_ref[i : i + 1, :])
            which = wide(source_ref[i : i + 1, :])
            half = [jnp.zeros((SUBLANES, LANES), jnp.float32)] * groups
            for s in range(sources):
                here = which == s
                for q in range(groups):
                    part = curves_ref[s, q * SUBLANES : (q + 1) * SUBLANES, :]
                    half[q] = jnp.where(here, lane_gather(part, lane), half[q])
            halves.append(half)
        return [jnp.concatenate([h[q] for h in halves], axis=1) for q in range(groups)]

    for t in range(assets // width):
        curves = jnp.concatenate(by_product(t) if t < PRODUCTS else by_gather(t), axis=0)
        following = jnp.concatenate([curves[1:], jnp.zeros((1, width), jnp.float32)], axis=0)
        change_ref[:, t * width : (t + 1) * width] = curves - following
    for t in range(assets // width):
        across = slice(t * width, (t + 1) * width)
        kinds = jnp.concatenate([class_ref[i : i + 1, :] for i in (2 * t, 2 * t + 1)], axis=1)
        match = lax.broadcasted_iota(jnp.int32, (classes, width), 0) == kinds
        onehot = jnp.where(match, 1.0, 0.0).astype(jnp.bfloat16)
        both = jnp.concatenate([onehot, onehot], axis=0)
        chosen = jnp.dot(split_ref[...], both, preferred_element_type=jnp.float32)
        total = jnp.zeros((bins, width), jnp.float32)
        for l in range(levels):
            part = chosen[l * bins : (l + 1) * bins, :]
            total = total + change_ref[l : l + 1, across] * part
        out_ref[:, across] = total


def per_device(
    site_x,
    site_y,
    site_amp,
    rup_x,
    rup_y,
    rup_mag,
    rup_rate,
    rup_source,
    src_sigma,
    src_shift,
    relay_sites,
    relay_count,
    asset_source,
    asset_pick,
    asset_class,
    vulnerability,
    rows,
    columns,
):
    classes, levels, bins = vulnerability.shape
    sites = site_x.shape[0]
    sources, capacity = relay_sites.shape[2:]
    assets = asset_source.shape[0]
    own_sites = sites // rows
    limit = pltpu.CompilerParams(vmem_limit_bytes=48 * 2**20)

    line = lambda a: a.reshape(1, -1)
    square = lambda a: a.reshape(-1, LANES)
    tiles = own_sites // LANES
    packed = pl.pallas_call(
        pack_kernel,
        out_shape=jax.ShapeDtypeStruct((rows, SUBLANES, LANES), jnp.float32),
        in_specs=[VMEM] * 6,
        out_specs=VMEM,
    )(
        line(rup_x),
        line(rup_y),
        line(rup_mag),
        line(rup_rate),
        line(rup_source),
        relay_sites[0, 0],
    )
    units = rows * LANES // SUBLANES
    sums_shape = (tiles * levels, SUBLANES, LANES)
    own, sums = pl.pallas_call(
        functools.partial(own_kernel, levels),
        out_shape=(
            jax.ShapeDtypeStruct((3 * tiles + 2, LANES), jnp.float32),
            jax.ShapeDtypeStruct(sums_shape, jnp.float32),
        ),
        in_specs=[VMEM] * 6,
        out_specs=(VMEM, VMEM),
        scratch_shapes=[pltpu.VMEM((2 + tiles, units // rows, SUBLANES, LANES), jnp.float32)],
        compiler_params=limit,
    )(
        packed,
        square(site_x),
        square(site_y),
        square(site_amp),
        line(src_sigma),
        line(src_shift),
    )
    groups = [[j * columns + partner(0, d, j) for j in range(rows)] for d in range(columns)]
    ruptures = lax.all_to_all(packed, ("rup", "site"), 0, 0, axis_index_groups=groups, tiled=True)
    heights = 4
    length = tiles * levels
    copy = jax.ShapeDtypeStruct((length + SUBLANES, LANES), jnp.float32)
    copies = pl.pallas_call(
        functools.partial(hazard_kernel, levels),
        out_shape=(copy,) * heights,
        in_specs=[VMEM] * 3,
        out_specs=(VMEM,) * heights,
        scratch_shapes=[
            pltpu.VMEM((2 + tiles, units, SUBLANES, LANES), jnp.float32),
            pltpu.VMEM(sums_shape, jnp.float32),
        ],
        compiler_params=limit,
    )(own, sums, ruptures)
    swap = lambda k: lax.ppermute(copies[k], "rup", [(r, r ^ k) for r in range(rows)])
    east = rows // heights
    merged = pl.pallas_call(
        functools.partial(merge_kernel, heights),
        out_shape=(jax.ShapeDtypeStruct((heights * length + SUBLANES, LANES), jnp.float32),) * east,
        in_specs=[VMEM] * heights,
        out_specs=(VMEM,) * east,
        compiler_params=limit,
    )(copies[0], *[swap(k) for k in range(1, heights)])
    shift = lambda k: lax.ppermute(
        merged[k], "rup", [(r, r ^ (k * heights)) for r in range(rows)]
    )
    parts = [merged[0]] + [shift(k) for k in range(1, east)]
    hazard = pl.pallas_call(
        functools.partial(output_kernel, levels),
        out_shape=jax.ShapeDtypeStruct((levels, sites), jnp.float32),
        in_specs=[VMEM] * east,
        out_specs=VMEM,
        compiler_params=limit,
    )(*parts)
    send = pl.pallas_call(
        functools.partial(relay_kernel, levels, own_sites),
        out_shape=jax.ShapeDtypeStruct((columns, levels, capacity), jnp.float32),
        in_specs=[VMEM] * east,
        out_specs=VMEM,
        scratch_shapes=[pltpu.VMEM((rows * levels, 3 * own_sites), jnp.bfloat16)],
        compiler_params=limit,
    )(*parts)
    curves = lax.all_to_all(send, "site", 0, 0, tiled=True)
    table = jnp.transpose(vulnerability, (1, 2, 0)).reshape(levels * bins, classes)
    slot, split = pl.pallas_call(
        table_kernel,
        out_shape=(
            jax.ShapeDtypeStruct((assets // LANES, LANES), jnp.int32),
            jax.ShapeDtypeStruct((levels * bins, 2 * classes), jnp.bfloat16),
        ),
        in_specs=[VMEM, VMEM, SMEM, VMEM],
        out_specs=(VMEM, VMEM),
        compiler_params=limit,
    )(square(asset_source), square(asset_pick), relay_count.reshape(1, sources), table)
    losses = pl.pallas_call(
        loss_kernel,
        out_shape=jax.ShapeDtypeStruct((bins, assets), jnp.float32),
        in_specs=[VMEM] * 5,
        out_specs=VMEM,
        scratch_shapes=[
            pltpu.VMEM((sources * levels // 2, 6 * LANES), jnp.bfloat16),
            pltpu.VMEM((levels, assets), jnp.float32),
        ],
        compiler_params=limit,
    )(curves, square(asset_source), slot, square(asset_class), split)
    return hazard, losses


def solution(mesh):
    return jax.shard_map(
        functools.partial(per_device, rows=mesh.shape["rup"], columns=mesh.shape["site"]),
        mesh=mesh,
        in_specs=(
            P("site"),
            P("site"),
            P("site"),
            P("rup"),
            P("rup"),
            P("rup"),
            P("rup"),
            P("rup"),
            P(),
            P(),
            P("rup", "site", None, None),
            P("rup", "site", None),
            P(("rup", "site")),
            P(("rup", "site")),
            P(("rup", "site")),
            P(),
        ),
        out_specs=(P(None, "site"), P(None, ("rup", "site"))),
        check_vma=False,
    )
```

```python
import functools
import math

import jax
import jax.numpy as jnp
from jax import lax
from jax.experimental import pallas as pl
from jax.experimental.pallas import tpu as pltpu
from jax.sharding import PartitionSpec as P

LANES = 128
SUBLANES = 8
LIST = 5
FAR_FIRST = (0, 2, 1, 3)
UNROLL = 24
PRODUCTS = 2
VMEM = pl.BlockSpec(memory_space=pltpu.VMEM)
SMEM = pl.BlockSpec(memory_space=pltpu.SMEM)
LEVEL_FIRST = math.log(0.005)
LEVEL_RANGE = math.log(600.0)


def lane_gather(row, index):
    return jnp.take_along_axis(row, index, axis=1, mode="promise_in_bounds")


def partner(row, site, other):
    inner = lambda r: (((r & 3) + 1) >> 1) & 1
    south = lambda r: 2 * inner(r) - (r >> 2)
    z_lo = (site >> 3) ^ inner(row) ^ inner(other)
    y = (((site >> 1) & 3) - south(row) + south(other)) & 3
    core = (site & 1) ^ ((row & 3) >> 1) ^ ((other & 3) >> 1)
    return z_lo * 8 + y * 2 + core


def place():
    return lax.axis_index("rup"), lax.axis_index("site")


def split_in_three(value):
    high = value.astype(jnp.bfloat16)
    rest = value - high.astype(jnp.float32)
    middle = rest.astype(jnp.bfloat16)
    return high, middle, (rest - middle.astype(jnp.float32)).astype(jnp.bfloat16)


def pack_kernel(x_ref, y_ref, mag_ref, rate_ref, source_ref, relay_ref, out_ref):
    row, site = place()
    source = source_ref[...].astype(jnp.float32)
    zero = jnp.zeros((1, LANES), jnp.float32)
    packed = jnp.concatenate(
        [x_ref[...], y_ref[...], mag_ref[...], rate_ref[...], source, zero, zero, zero], axis=0
    )
    for j in range(out_ref.shape[0]):
        out_ref[j] = packed
        wanted = relay_ref[pl.ds(partner(row, site, j), 1), :]
        out_ref[j, LIST : LIST + 1, :] = wanted.astype(jnp.float32)


def wide(row):
    return jnp.broadcast_to(row, (SUBLANES, LANES))


def spreading():
    part = lax.broadcasted_iota(jnp.int32, (4 * SUBLANES, 5 * LANES), 0)
    which = lax.broadcasted_iota(jnp.int32, (4 * SUBLANES, 5 * LANES), 1) >> 7
    chosen = (part < 3 * SUBLANES) & ((part & (SUBLANES - 1)) == which)
    return jnp.where(chosen, 1.0, 0.0).astype(jnp.bfloat16)


def prepare(raw, at, levels, own_ref, spread_out, pre_ref):
    tiles = pre_ref.shape[0] - 2
    units = LANES // SUBLANES
    step = LEVEL_RANGE / (levels - 1)
    index = wide(raw[4:5]).astype(jnp.int32)
    sigma = wide(own_ref[3 * tiles : 3 * tiles + 1, :])
    shift = wide(own_ref[3 * tiles + 1 : 3 * tiles + 2, :])
    inverse = 1.0 / (lane_gather(sigma, index)[0:1] * math.sqrt(2.0))
    base = -1.0 + (raw[2:3] - 6.5) + lane_gather(shift, index)[0:1]
    zero = jnp.zeros((3, LANES), jnp.float32)
    rows = jnp.concatenate([raw[0:2], base, inverse, 0.5 * raw[3:4], zero], axis=0)
    thirds = [third.astype(jnp.float32) for third in split_in_three(rows)]
    stack = jnp.concatenate(thirds + [jnp.zeros_like(rows)], axis=0).astype(jnp.bfloat16)
    columns = lax.dot_general(
        stack, spread_out, (((0,), (0,)), ((), ())), preferred_element_type=jnp.float32
    )
    sites = [[wide(own_ref[i * tiles + t : i * tiles + t + 1, :]) for i in range(3)] for t in range(tiles)]
    for u in range(units):
        x, y, base, inverse, rate = [
            columns[u * SUBLANES : (u + 1) * SUBLANES, p * LANES : (p + 1) * LANES]
            for p in range(5)
        ]
        k = at * units + u
        pre_ref[0, k] = rate
        pre_ref[1, k] = inverse * step
        for t in range(tiles):
            site_x, site_y, amp = sites[t]
            dx = site_x - x
            dy = site_y - y
            median = base + amp - 0.6 * jnp.log((dx * dx + dy * dy + 100.0) * 0.01)
            pre_ref[2 + t, k] = (LEVEL_FIRST - median) * inverse


def tails(first, count, t, levels, pre_ref):
    total = [None] * levels
    for u in range(count):
        rate = pre_ref[0, first + u]
        gap = pre_ref[1, first + u]
        start = pre_ref[2 + t, first + u]
        whole = rate if u == 0 else whole + rate
        for l in range(levels):
            z = z + gap if l % 16 else start + gap * float(l)
            term = rate * lax.erf(z)
            total[l] = term if u == 0 else total[l] + term
    return [whole - part for part in total]


def own_kernel(
    levels, rup_ref, sx_ref, sy_ref, amp_ref, sigma_ref, shift_ref, own_ref, acc_ref, pre_ref
):
    rows = rup_ref.shape[0]
    row = place()[0]
    tiles = sx_ref.shape[0] // rows
    for i, ref in enumerate((sx_ref, sy_ref, amp_ref)):
        own_ref[i * tiles : (i + 1) * tiles, :] = ref[pl.ds(row * tiles, tiles), :]
    sources = sigma_ref.shape[1]
    own_ref[3 * tiles : 3 * tiles + 2, :] = jnp.zeros((2, LANES), jnp.float32)
    own_ref[3 * tiles : 3 * tiles + 1, 0:sources] = sigma_ref[...]
    own_ref[3 * tiles + 1 : 3 * tiles + 2, 0:sources] = shift_ref[...]
    prepare(rup_ref[0], 0, levels, own_ref, spreading(), pre_ref)
    for t in range(tiles):
        sums = tails(0, LANES // SUBLANES, t, levels, pre_ref)
        for l in range(levels):
            acc_ref[t * levels + l] = sums[l]


def hazard_kernel(levels, own_ref, sums_ref, rup_ref, *refs):
    out_refs, pre_ref, acc_ref = refs[:-2], refs[-2], refs[-1]
    blocks = rup_ref.shape[0]
    heights = len(out_refs)
    tiles = out_refs[0].shape[0] // levels
    units = LANES // SUBLANES
    row = place()[0]
    spread_out = spreading()
    acc_ref[...] = sums_ref[...]
    others = blocks - 1
    together = 5

    def prepare_some(g, carry):
        for i in range(together):
            at = g * together + i
            block = (row + 1 + at) & (blocks - 1)
            prepare(rup_ref[block], at, levels, own_ref, spread_out, pre_ref)
        return carry

    lax.fori_loop(0, others // together, prepare_some, 0)
    unroll = UNROLL

    for t in range(tiles):

        def add(g, carry):
            sums = tails(g * unroll, unroll, t, levels, pre_ref)
            for l in range(levels):
                at = t * levels + l
                acc_ref[at] = acc_ref[at] + sums[l]
            return carry

        lax.fori_loop(0, others * units // unroll, add, 0)
    for t in range(tiles):
        for q in range(0, levels, SUBLANES):
            rates = jnp.concatenate(
                [
                    jnp.sum(acc_ref[t * levels + l], axis=0, keepdims=True)
                    for l in range(q, q + SUBLANES)
                ],
                axis=0,
            )
            hazard = 1.0 - jnp.exp(-rates)
            for out_ref in out_refs:
                out_ref[t * levels + q : t * levels + q + SUBLANES, :] = hazard
    for k, out_ref in enumerate(out_refs):
        height = (row & (heights - 1)) ^ k
        lists = [rup_ref[x * heights + height, LIST : LIST + 1, :] for x in range(blocks // heights)]
        lists.append(jnp.zeros((SUBLANES - len(lists), LANES), jnp.float32))
        out_ref[tiles * levels :, :] = jnp.concatenate(lists, axis=0)


def merge_kernel(heights, *refs):
    in_refs, out_refs = refs[:heights], refs[heights:]
    length = in_refs[0].shape[0] - SUBLANES
    row = place()[0]
    for k, out_ref in enumerate(out_refs):
        x = (row >> 2) ^ k
        out_ref[heights * length :, :] = jnp.zeros((SUBLANES, LANES), jnp.float32)
        for flip, in_ref in zip(FAR_FIRST, in_refs):
            height = (row & (heights - 1)) ^ flip
            at = pl.multiple_of(height * length, length)
            out_ref[pl.ds(at, length), :] = in_ref[0:length, :]
            out_ref[pl.ds(heights * length + height, 1), :] = in_ref[pl.ds(length + x, 1), :]


def output_kernel(levels, *refs):
    in_refs, out_ref = refs[:-1], refs[-1]
    row = place()[0]
    tiles = out_ref.shape[1] // (len(in_refs) * LANES)
    for k, in_ref in zip(FAR_FIRST, in_refs):
        x = (row >> 2) ^ k
        for t in range(tiles):
            at = pl.multiple_of((x * tiles + t) * LANES, LANES)
            out_ref[:, pl.ds(at, LANES)] = in_ref[t * levels : (t + 1) * levels, :]


def pick_by_product(lhs_ref, levels, index):
    span = lhs_ref.shape[1] // 3
    blocks = lhs_ref.shape[0] // levels
    width = index.shape[1]
    low = index & (span - 1)
    high = jnp.broadcast_to(index >> (span.bit_length() - 1), (SUBLANES, width))
    match = lax.broadcasted_iota(jnp.int32, (span, width), 0) == low
    onehot = jnp.where(match, 1.0, 0.0).astype(jnp.bfloat16)
    found = jnp.dot(
        lhs_ref[...],
        jnp.concatenate([onehot] * 3, axis=0),
        preferred_element_type=jnp.float32,
    )
    picked = [jnp.zeros((SUBLANES, width), jnp.float32)] * (levels // SUBLANES)
    for b in range(blocks):
        here = high == b
        for q in range(len(picked)):
            at = b * levels + q * SUBLANES
            picked[q] = jnp.where(here, found[at : at + SUBLANES], picked[q])
    return picked


def relay_kernel(levels, span, *refs):
    part_refs, send_ref, lhs_ref = [refs[k] for k in FAR_FIRST], refs[-2], refs[-1]
    parts = len(part_refs)
    heights = (part_refs[0].shape[0] - SUBLANES) * LANES // (levels * span)
    blocks = parts * heights
    groups = levels // SUBLANES
    tiles = span // LANES
    row, site = place()

    def origin(b):
        return ((row >> 2) ^ (b // heights)) * heights + b % heights

    def piece(b, t, first, count):
        at = (b % heights * tiles + t) * levels + first
        return part_refs[b // heights][at : at + count, :]

    def wanted(k):
        at = heights * tiles * levels + k % heights
        return part_refs[k // heights][at : at + 1, :].astype(jnp.int32)

    for b in range(blocks):
        for t in range(tiles):
            thirds = split_in_three(piece(b, t, 0, levels))
            for i in range(3):
                at = i * span + t * LANES
                first = pl.multiple_of(origin(b) * levels, levels)
                lhs_ref[pl.ds(first, levels), at : at + LANES] = thirds[i]

    def by_product(k):
        index = jnp.concatenate([wanted(k + i) for i in range(2)], axis=1)
        picked = pick_by_product(lhs_ref, levels, index)
        for i in range(2):
            owner = partner(origin(k + i), site, row)
            for q in range(groups):
                send_ref[owner, q * SUBLANES : (q + 1) * SUBLANES, :] = picked[q][
                    :, i * LANES : (i + 1) * LANES
                ]

    def by_gather(k):
        index = wide(wanted(k))
        lane = index & (LANES - 1)
        tile = index >> 7
        picked = [jnp.zeros((SUBLANES, LANES), jnp.float32)] * groups
        for c in range(blocks * tiles):
            b, t = c // tiles, c % tiles
            here = tile == origin(b) * tiles + t
            for q in range(groups):
                part = piece(b, t, q * SUBLANES, SUBLANES)
                picked[q] = jnp.where(here, lane_gather(part, lane), picked[q])
        owner = partner(origin(k), site, row)
        for q in range(groups):
            send_ref[owner, q * SUBLANES : (q + 1) * SUBLANES, :] = picked[q]

    products = blocks * 5 // 16
    for i in range(products):
        by_product(2 * i)
        by_gather(2 * products + i)
    for k in range(3 * products, blocks):
        by_gather(k)


def table_kernel(source_ref, pick_ref, count_ref, table_ref, slot_ref, split_ref):
    source = source_ref[...]
    count = jnp.zeros(source.shape, jnp.int32)
    for s in range(count_ref.shape[1]):
        count = jnp.where(source == s, count_ref[0, s], count)
    pick = pick_ref[...]
    quotient = jnp.floor(pick.astype(jnp.float32) / count.astype(jnp.float32)).astype(jnp.int32)
    slot = pick - quotient * count
    slot = jnp.where(slot < 0, slot + count, slot)
    slot_ref[...] = jnp.where(slot >= count, slot - count, slot)
    classes = table_ref.shape[1]
    table = table_ref[...]
    high = table.astype(jnp.bfloat16)
    split_ref[:, 0:classes] = high
    split_ref[:, classes : 2 * classes] = (table - high.astype(jnp.float32)).astype(jnp.bfloat16)


def loss_kernel(
    curves_ref, source_ref, slot_ref, class_ref, split_ref, out_ref, lhs_ref, change_ref
):
    sources, levels, _ = curves_ref.shape
    bins, assets = out_ref.shape
    classes = split_ref.shape[1] // 2
    groups = levels // SUBLANES
    width = 2 * LANES
    for s in range(sources):
        thirds = split_in_three(curves_ref[s])
        for i in range(3):
            at = i * width + (s % 2) * LANES
            lhs_ref[s // 2 * levels : (s // 2 + 1) * levels, at : at + LANES] = thirds[i]

    def by_product(t):
        index = jnp.concatenate(
            [source_ref[i : i + 1, :] * LANES + slot_ref[i : i + 1, :] for i in (2 * t, 2 * t + 1)],
            axis=1,
        )
        return pick_by_product(lhs_ref, levels, index)

    def by_gather(t):
        halves = []
        for i in (2 * t, 2 * t + 1):
            lane = wide(slot_ref[i : i + 1, :])
            which = wide(source_ref[i : i + 1, :])
            half = [jnp.zeros((SUBLANES, LANES), jnp.float32)] * groups
            for s in range(sources):
                here = which == s
                for q in range(groups):
                    part = curves_ref[s, q * SUBLANES : (q + 1) * SUBLANES, :]
                    half[q] = jnp.where(here, lane_gather(part, lane), half[q])
            halves.append(half)
        return [jnp.concatenate([h[q] for h in halves], axis=1) for q in range(groups)]

    for t in range(assets // width):
        curves = jnp.concatenate(by_product(t) if t < PRODUCTS else by_gather(t), axis=0)
        following = jnp.concatenate([curves[1:], jnp.zeros((1, width), jnp.float32)], axis=0)
        change_ref[:, t * width : (t + 1) * width] = curves - following
    for t in range(assets // width):
        across = slice(t * width, (t + 1) * width)
        kinds = jnp.concatenate([class_ref[i : i + 1, :] for i in (2 * t, 2 * t + 1)], axis=1)
        match = lax.broadcasted_iota(jnp.int32, (classes, width), 0) == kinds
        onehot = jnp.where(match, 1.0, 0.0).astype(jnp.bfloat16)
        both = jnp.concatenate([onehot, onehot], axis=0)
        chosen = jnp.dot(split_ref[...], both, preferred_element_type=jnp.float32)
        total = jnp.zeros((bins, width), jnp.float32)
        for l in range(levels):
            part = chosen[l * bins : (l + 1) * bins, :]
            total = total + change_ref[l : l + 1, across] * part
        out_ref[:, across] = total


def per_device(
    site_x,
    site_y,
    site_amp,
    rup_x,
    rup_y,
    rup_mag,
    rup_rate,
    rup_source,
    src_sigma,
    src_shift,
    relay_sites,
    relay_count,
    asset_source,
    asset_pick,
    asset_class,
    vulnerability,
    rows,
    columns,
):
    classes, levels, bins = vulnerability.shape
    sites = site_x.shape[0]
    sources, capacity = relay_sites.shape[2:]
    assets = asset_source.shape[0]
    own_sites = sites // rows
    limit = pltpu.CompilerParams(vmem_limit_bytes=48 * 2**20)

    line = lambda a: a.reshape(1, -1)
    square = lambda a: a.reshape(-1, LANES)
    tiles = own_sites // LANES
    packed = pl.pallas_call(
        pack_kernel,
        out_shape=jax.ShapeDtypeStruct((rows, SUBLANES, LANES), jnp.float32),
        in_specs=[VMEM] * 6,
        out_specs=VMEM,
    )(
        line(rup_x),
        line(rup_y),
        line(rup_mag),
        line(rup_rate),
        line(rup_source),
        relay_sites[0, 0],
    )
    units = rows * LANES // SUBLANES
    sums_shape = (tiles * levels, SUBLANES, LANES)
    own, sums = pl.pallas_call(
        functools.partial(own_kernel, levels),
        out_shape=(
            jax.ShapeDtypeStruct((3 * tiles + 2, LANES), jnp.float32),
            jax.ShapeDtypeStruct(sums_shape, jnp.float32),
        ),
        in_specs=[VMEM] * 6,
        out_specs=(VMEM, VMEM),
        scratch_shapes=[pltpu.VMEM((2 + tiles, units // rows, SUBLANES, LANES), jnp.float32)],
        compiler_params=limit,
    )(
        packed,
        square(site_x),
        square(site_y),
        square(site_amp),
        line(src_sigma),
        line(src_shift),
    )
    groups = [[j * columns + partner(0, d, j) for j in range(rows)] for d in range(columns)]
    ruptures = lax.all_to_all(packed, ("rup", "site"), 0, 0, axis_index_groups=groups, tiled=True)
    heights = 4
    length = tiles * levels
    copy = jax.ShapeDtypeStruct((length + SUBLANES, LANES), jnp.float32)
    copies = pl.pallas_call(
        functools.partial(hazard_kernel, levels),
        out_shape=(copy,) * heights,
        in_specs=[VMEM] * 3,
        out_specs=(VMEM,) * heights,
        scratch_shapes=[
            pltpu.VMEM((2 + tiles, units, SUBLANES, LANES), jnp.float32),
            pltpu.VMEM(sums_shape, jnp.float32),
        ],
        compiler_params=limit,
    )(own, sums, ruptures)
    swap = lambda k: lax.ppermute(copies[k], "rup", [(r, r ^ k) for r in range(rows)])
    east = rows // heights
    merged = pl.pallas_call(
        functools.partial(merge_kernel, heights),
        out_shape=(jax.ShapeDtypeStruct((heights * length + SUBLANES, LANES), jnp.float32),) * east,
        in_specs=[VMEM] * heights,
        out_specs=(VMEM,) * east,
        compiler_params=limit,
    )(*[swap(k) if k else copies[0] for k in FAR_FIRST])
    shift = lambda k: lax.ppermute(
        merged[k], "rup", [(r, r ^ (k * heights)) for r in range(rows)]
    )
    parts = [shift(k) if k else merged[0] for k in FAR_FIRST]
    hazard = pl.pallas_call(
        functools.partial(output_kernel, levels),
        out_shape=jax.ShapeDtypeStruct((levels, sites), jnp.float32),
        in_specs=[VMEM] * east,
        out_specs=VMEM,
        compiler_params=limit,
    )(*parts)
    send = pl.pallas_call(
        functools.partial(relay_kernel, levels, own_sites),
        out_shape=jax.ShapeDtypeStruct((columns, levels, capacity), jnp.float32),
        in_specs=[VMEM] * east,
        out_specs=VMEM,
        scratch_shapes=[pltpu.VMEM((rows * levels, 3 * own_sites), jnp.bfloat16)],
        compiler_params=limit,
    )(*parts)
    curves = lax.all_to_all(send, "site", 0, 0, tiled=True)
    table = jnp.transpose(vulnerability, (1, 2, 0)).reshape(levels * bins, classes)
    slot, split = pl.pallas_call(
        table_kernel,
        out_shape=(
            jax.ShapeDtypeStruct((assets // LANES, LANES), jnp.int32),
            jax.ShapeDtypeStruct((levels * bins, 2 * classes), jnp.bfloat16),
        ),
        in_specs=[VMEM, VMEM, SMEM, VMEM],
        out_specs=(VMEM, VMEM),
        compiler_params=limit,
    )(square(asset_source), square(asset_pick), relay_count.reshape(1, sources), table)
    losses = pl.pallas_call(
        loss_kernel,
        out_shape=jax.ShapeDtypeStruct((bins, assets), jnp.float32),
        in_specs=[VMEM] * 5,
        out_specs=VMEM,
        scratch_shapes=[
            pltpu.VMEM((sources * levels // 2, 6 * LANES), jnp.bfloat16),
            pltpu.VMEM((levels, assets), jnp.float32),
        ],
        compiler_params=limit,
    )(curves, square(asset_source), slot, square(asset_class), split)
    return hazard, losses


def solution(mesh):
    return jax.shard_map(
        functools.partial(per_device, rows=mesh.shape["rup"], columns=mesh.shape["site"]),
        mesh=mesh,
        in_specs=(
            P("site"),
            P("site"),
            P("site"),
            P("rup"),
            P("rup"),
            P("rup"),
            P("rup"),
            P("rup"),
            P(),
            P(),
            P("rup", "site", None, None),
            P("rup", "site", None),
            P(("rup", "site")),
            P(("rup", "site")),
            P(("rup", "site")),
            P(),
        ),
        out_specs=(P(None, "site"), P(None, ("rup", "site"))),
        check_vma=False,
    )
```

```python
import functools
import math

import jax
import jax.numpy as jnp
from jax import lax
from jax.experimental import pallas as pl
from jax.experimental.pallas import tpu as pltpu
from jax.sharding import PartitionSpec as P

LANES = 128
SUBLANES = 8
LIST = 5
FAR_FIRST = (0, 2, 1, 3)
UNROLL = 24
PRODUCTS = 2
VMEM = pl.BlockSpec(memory_space=pltpu.VMEM)
SMEM = pl.BlockSpec(memory_space=pltpu.SMEM)
LEVEL_FIRST = math.log(0.005)
LEVEL_RANGE = math.log(600.0)


def lane_gather(row, index):
    return jnp.take_along_axis(row, index, axis=1, mode="promise_in_bounds")


def partner(row, site, other):
    inner = lambda r: (((r & 3) + 1) >> 1) & 1
    south = lambda r: 2 * inner(r) - (r >> 2)
    z_lo = (site >> 3) ^ inner(row) ^ inner(other)
    y = (((site >> 1) & 3) - south(row) + south(other)) & 3
    core = (site & 1) ^ ((row & 3) >> 1) ^ ((other & 3) >> 1)
    return z_lo * 8 + y * 2 + core


def place():
    return lax.axis_index("rup"), lax.axis_index("site")


def split_in_three(value):
    high = value.astype(jnp.bfloat16)
    rest = value - high.astype(jnp.float32)
    middle = rest.astype(jnp.bfloat16)
    return high, middle, (rest - middle.astype(jnp.float32)).astype(jnp.bfloat16)


def pack_kernel(*refs):
    count = 6
    out_ref, semaphores = refs[count], refs[-1]
    x_ref, y_ref, mag_ref, rate_ref, source_ref, relay_ref = refs[count + 1 : -1]
    copies = [
        pltpu.make_async_copy(refs[i], refs[count + 1 + i], semaphores.at[i]) for i in range(count)
    ]
    for copy in copies:
        copy.start()
    for copy in copies:
        copy.wait()
    row, site = place()
    source = source_ref[...].astype(jnp.float32)
    zero = jnp.zeros((1, LANES), jnp.float32)
    packed = jnp.concatenate(
        [x_ref[...], y_ref[...], mag_ref[...], rate_ref[...], source, zero, zero, zero], axis=0
    )
    for j in range(out_ref.shape[0]):
        out_ref[j] = packed
        wanted = relay_ref[pl.ds(partner(row, site, j), 1), :]
        out_ref[j, LIST : LIST + 1, :] = wanted.astype(jnp.float32)


def wide(row):
    return jnp.broadcast_to(row, (SUBLANES, LANES))


def spreading():
    part = lax.broadcasted_iota(jnp.int32, (4 * SUBLANES, 5 * LANES), 0)
    which = lax.broadcasted_iota(jnp.int32, (4 * SUBLANES, 5 * LANES), 1) >> 7
    chosen = (part < 3 * SUBLANES) & ((part & (SUBLANES - 1)) == which)
    return jnp.where(chosen, 1.0, 0.0).astype(jnp.bfloat16)


def prepare(raw, at, levels, own_ref, spread_out, pre_ref):
    tiles = pre_ref.shape[0] - 2
    units = LANES // SUBLANES
    step = LEVEL_RANGE / (levels - 1)
    index = wide(raw[4:5]).astype(jnp.int32)
    sigma = wide(own_ref[3 * tiles : 3 * tiles + 1, :])
    shift = wide(own_ref[3 * tiles + 1 : 3 * tiles + 2, :])
    inverse = 1.0 / (lane_gather(sigma, index)[0:1] * math.sqrt(2.0))
    base = -1.0 + (raw[2:3] - 6.5) + lane_gather(shift, index)[0:1]
    zero = jnp.zeros((3, LANES), jnp.float32)
    rows = jnp.concatenate([raw[0:2], base, inverse, 0.5 * raw[3:4], zero], axis=0)
    thirds = [third.astype(jnp.float32) for third in split_in_three(rows)]
    stack = jnp.concatenate(thirds + [jnp.zeros_like(rows)], axis=0).astype(jnp.bfloat16)
    columns = lax.dot_general(
        stack, spread_out, (((0,), (0,)), ((), ())), preferred_element_type=jnp.float32
    )
    sites = [[wide(own_ref[i * tiles + t : i * tiles + t + 1, :]) for i in range(3)] for t in range(tiles)]
    for u in range(units):
        x, y, base, inverse, rate = [
            columns[u * SUBLANES : (u + 1) * SUBLANES, p * LANES : (p + 1) * LANES]
            for p in range(5)
        ]
        k = at * units + u
        pre_ref[0, k] = rate
        pre_ref[1, k] = inverse * step
        for t in range(tiles):
            site_x, site_y, amp = sites[t]
            dx = site_x - x
            dy = site_y - y
            median = base + amp - 0.6 * jnp.log((dx * dx + dy * dy + 100.0) * 0.01)
            pre_ref[2 + t, k] = (LEVEL_FIRST - median) * inverse


def tails(first, count, t, levels, pre_ref):
    total = [None] * levels
    for u in range(count):
        rate = pre_ref[0, first + u]
        gap = pre_ref[1, first + u]
        start = pre_ref[2 + t, first + u]
        whole = rate if u == 0 else whole + rate
        for l in range(levels):
            z = z + gap if l % 16 else start + gap * float(l)
            term = rate * lax.erf(z)
            total[l] = term if u == 0 else total[l] + term
    return [whole - part for part in total]


def own_kernel(
    levels, rup_ref, sx_ref, sy_ref, amp_ref, sigma_ref, shift_ref, own_ref, acc_ref, pre_ref
):
    rows = rup_ref.shape[0]
    row = place()[0]
    tiles = sx_ref.shape[0] // rows
    for i, ref in enumerate((sx_ref, sy_ref, amp_ref)):
        own_ref[i * tiles : (i + 1) * tiles, :] = ref[pl.ds(row * tiles, tiles), :]
    sources = sigma_ref.shape[1]
    own_ref[3 * tiles : 3 * tiles + 2, :] = jnp.zeros((2, LANES), jnp.float32)
    own_ref[3 * tiles : 3 * tiles + 1, 0:sources] = sigma_ref[...]
    own_ref[3 * tiles + 1 : 3 * tiles + 2, 0:sources] = shift_ref[...]
    prepare(rup_ref[0], 0, levels, own_ref, spreading(), pre_ref)
    for t in range(tiles):
        sums = tails(0, LANES // SUBLANES, t, levels, pre_ref)
        for l in range(levels):
            acc_ref[t * levels + l] = sums[l]


def hazard_kernel(levels, own_ref, sums_ref, rup_ref, *refs):
    out_refs, pre_ref, acc_ref = refs[:-2], refs[-2], refs[-1]
    blocks = rup_ref.shape[0]
    heights = len(out_refs)
    tiles = out_refs[0].shape[0] // levels
    units = LANES // SUBLANES
    row = place()[0]
    spread_out = spreading()
    acc_ref[...] = sums_ref[...]
    others = blocks - 1
    together = 5

    def prepare_some(g, carry):
        for i in range(together):
            at = g * together + i
            block = (row + 1 + at) & (blocks - 1)
            prepare(rup_ref[block], at, levels, own_ref, spread_out, pre_ref)
        return carry

    lax.fori_loop(0, others // together, prepare_some, 0)
    unroll = UNROLL

    for t in range(tiles):

        def add(g, carry):
            sums = tails(g * unroll, unroll, t, levels, pre_ref)
            for l in range(levels):
                at = t * levels + l
                acc_ref[at] = acc_ref[at] + sums[l]
            return carry

        lax.fori_loop(0, others * units // unroll, add, 0)
    for t in range(tiles):
        for q in range(0, levels, SUBLANES):
            rates = jnp.concatenate(
                [
                    jnp.sum(acc_ref[t * levels + l], axis=0, keepdims=True)
                    for l in range(q, q + SUBLANES)
                ],
                axis=0,
            )
            hazard = 1.0 - jnp.exp(-rates)
            for out_ref in out_refs:
                out_ref[t * levels + q : t * levels + q + SUBLANES, :] = hazard
    for k, out_ref in enumerate(out_refs):
        height = (row & (heights - 1)) ^ k
        lists = [rup_ref[x * heights + height, LIST : LIST + 1, :] for x in range(blocks // heights)]
        lists.append(jnp.zeros((SUBLANES - len(lists), LANES), jnp.float32))
        out_ref[tiles * levels :, :] = jnp.concatenate(lists, axis=0)


def merge_kernel(heights, *refs):
    in_refs, out_refs = refs[:heights], refs[heights:]
    length = in_refs[0].shape[0] - SUBLANES
    row = place()[0]
    for k, out_ref in enumerate(out_refs):
        x = (row >> 2) ^ k
        out_ref[heights * length :, :] = jnp.zeros((SUBLANES, LANES), jnp.float32)
        for flip, in_ref in zip(FAR_FIRST, in_refs):
            height = (row & (heights - 1)) ^ flip
            at = pl.multiple_of(height * length, length)
            out_ref[pl.ds(at, length), :] = in_ref[0:length, :]
            out_ref[pl.ds(heights * length + height, 1), :] = in_ref[pl.ds(length + x, 1), :]


def output_kernel(levels, *refs):
    in_refs, out_ref = refs[:-1], refs[-1]
    row = place()[0]
    tiles = out_ref.shape[1] // (len(in_refs) * LANES)
    for k, in_ref in zip(FAR_FIRST, in_refs):
        x = (row >> 2) ^ k
        for t in range(tiles):
            at = pl.multiple_of((x * tiles + t) * LANES, LANES)
            out_ref[:, pl.ds(at, LANES)] = in_ref[t * levels : (t + 1) * levels, :]


def pick_by_product(lhs_ref, levels, index):
    span = lhs_ref.shape[1] // 3
    blocks = lhs_ref.shape[0] // levels
    width = index.shape[1]
    low = index & (span - 1)
    high = jnp.broadcast_to(index >> (span.bit_length() - 1), (SUBLANES, width))
    match = lax.broadcasted_iota(jnp.int32, (span, width), 0) == low
    onehot = jnp.where(match, 1.0, 0.0).astype(jnp.bfloat16)
    found = jnp.dot(
        lhs_ref[...],
        jnp.concatenate([onehot] * 3, axis=0),
        preferred_element_type=jnp.float32,
    )
    picked = [jnp.zeros((SUBLANES, width), jnp.float32)] * (levels // SUBLANES)
    for b in range(blocks):
        here = high == b
        for q in range(len(picked)):
            at = b * levels + q * SUBLANES
            picked[q] = jnp.where(here, found[at : at + SUBLANES], picked[q])
    return picked


def relay_kernel(levels, span, *refs):
    part_refs, send_ref, lhs_ref = [refs[k] for k in FAR_FIRST], refs[-2], refs[-1]
    parts = len(part_refs)
    heights = (part_refs[0].shape[0] - SUBLANES) * LANES // (levels * span)
    blocks = parts * heights
    groups = levels // SUBLANES
    tiles = span // LANES
    row, site = place()

    def origin(b):
        return ((row >> 2) ^ (b // heights)) * heights + b % heights

    def piece(b, t, first, count):
        at = (b % heights * tiles + t) * levels + first
        return part_refs[b // heights][at : at + count, :]

    def wanted(k):
        at = heights * tiles * levels + k % heights
        return part_refs[k // heights][at : at + 1, :].astype(jnp.int32)

    for b in range(blocks):
        for t in range(tiles):
            thirds = split_in_three(piece(b, t, 0, levels))
            for i in range(3):
                at = i * span + t * LANES
                first = pl.multiple_of(origin(b) * levels, levels)
                lhs_ref[pl.ds(first, levels), at : at + LANES] = thirds[i]

    def by_product(k):
        index = jnp.concatenate([wanted(k + i) for i in range(2)], axis=1)
        picked = pick_by_product(lhs_ref, levels, index)
        for i in range(2):
            owner = partner(origin(k + i), site, row)
            for q in range(groups):
                send_ref[owner, q * SUBLANES : (q + 1) * SUBLANES, :] = picked[q][
                    :, i * LANES : (i + 1) * LANES
                ]

    def by_gather(k):
        index = wide(wanted(k))
        lane = index & (LANES - 1)
        tile = index >> 7
        picked = [jnp.zeros((SUBLANES, LANES), jnp.float32)] * groups
        for c in range(blocks * tiles):
            b, t = c // tiles, c % tiles
            here = tile == origin(b) * tiles + t
            for q in range(groups):
                part = piece(b, t, q * SUBLANES, SUBLANES)
                picked[q] = jnp.where(here, lane_gather(part, lane), picked[q])
        owner = partner(origin(k), site, row)
        for q in range(groups):
            send_ref[owner, q * SUBLANES : (q + 1) * SUBLANES, :] = picked[q]

    products = blocks * 5 // 16
    for i in range(products):
        by_product(2 * i)
        by_gather(2 * products + i)
    for k in range(3 * products, blocks):
        by_gather(k)


def table_kernel(source_ref, pick_ref, count_ref, table_ref, slot_ref, split_ref):
    source = source_ref[...]
    count = jnp.zeros(source.shape, jnp.int32)
    for s in range(count_ref.shape[1]):
        count = jnp.where(source == s, count_ref[0, s], count)
    pick = pick_ref[...]
    quotient = jnp.floor(pick.astype(jnp.float32) / count.astype(jnp.float32)).astype(jnp.int32)
    slot = pick - quotient * count
    slot = jnp.where(slot < 0, slot + count, slot)
    slot_ref[...] = jnp.where(slot >= count, slot - count, slot)
    classes = table_ref.shape[1]
    table = table_ref[...]
    high = table.astype(jnp.bfloat16)
    split_ref[:, 0:classes] = high
    split_ref[:, classes : 2 * classes] = (table - high.astype(jnp.float32)).astype(jnp.bfloat16)


def loss_kernel(
    curves_ref, source_ref, slot_ref, class_ref, split_ref, out_ref, lhs_ref, change_ref
):
    sources, levels, _ = curves_ref.shape
    bins, assets = out_ref.shape
    classes = split_ref.shape[1] // 2
    groups = levels // SUBLANES
    width = 2 * LANES
    for s in range(sources):
        thirds = split_in_three(curves_ref[s])
        for i in range(3):
            at = i * width + (s % 2) * LANES
            lhs_ref[s // 2 * levels : (s // 2 + 1) * levels, at : at + LANES] = thirds[i]

    def by_product(t):
        index = jnp.concatenate(
            [source_ref[i : i + 1, :] * LANES + slot_ref[i : i + 1, :] for i in (2 * t, 2 * t + 1)],
            axis=1,
        )
        return pick_by_product(lhs_ref, levels, index)

    def by_gather(t):
        halves = []
        for i in (2 * t, 2 * t + 1):
            lane = wide(slot_ref[i : i + 1, :])
            which = wide(source_ref[i : i + 1, :])
            half = [jnp.zeros((SUBLANES, LANES), jnp.float32)] * groups
            for s in range(sources):
                here = which == s
                for q in range(groups):
                    part = curves_ref[s, q * SUBLANES : (q + 1) * SUBLANES, :]
                    half[q] = jnp.where(here, lane_gather(part, lane), half[q])
            halves.append(half)
        return [jnp.concatenate([h[q] for h in halves], axis=1) for q in range(groups)]

    for t in range(assets // width):
        curves = jnp.concatenate(by_product(t) if t < PRODUCTS else by_gather(t), axis=0)
        following = jnp.concatenate([curves[1:], jnp.zeros((1, width), jnp.float32)], axis=0)
        change_ref[:, t * width : (t + 1) * width] = curves - following
    for t in range(assets // width):
        across = slice(t * width, (t + 1) * width)
        kinds = jnp.concatenate([class_ref[i : i + 1, :] for i in (2 * t, 2 * t + 1)], axis=1)
        match = lax.broadcasted_iota(jnp.int32, (classes, width), 0) == kinds
        onehot = jnp.where(match, 1.0, 0.0).astype(jnp.bfloat16)
        both = jnp.concatenate([onehot, onehot], axis=0)
        chosen = jnp.dot(split_ref[...], both, preferred_element_type=jnp.float32)
        total = jnp.zeros((bins, width), jnp.float32)
        for l in range(levels):
            part = chosen[l * bins : (l + 1) * bins, :]
            total = total + change_ref[l : l + 1, across] * part
        out_ref[:, across] = total


def per_device(
    site_x,
    site_y,
    site_amp,
    rup_x,
    rup_y,
    rup_mag,
    rup_rate,
    rup_source,
    src_sigma,
    src_shift,
    relay_sites,
    relay_count,
    asset_source,
    asset_pick,
    asset_class,
    vulnerability,
    rows,
    columns,
):
    classes, levels, bins = vulnerability.shape
    sites = site_x.shape[0]
    sources, capacity = relay_sites.shape[2:]
    assets = asset_source.shape[0]
    own_sites = sites // rows
    limit = pltpu.CompilerParams(vmem_limit_bytes=48 * 2**20)

    line = lambda a: a.reshape(1, -1)
    square = lambda a: a.reshape(-1, LANES)
    tiles = own_sites // LANES
    packed = pl.pallas_call(
        pack_kernel,
        out_shape=jax.ShapeDtypeStruct((rows, SUBLANES, LANES), jnp.float32),
        in_specs=[pl.BlockSpec(memory_space=pltpu.HBM)] * 6,
        out_specs=VMEM,
        scratch_shapes=[pltpu.VMEM((1, LANES), jnp.float32)] * 4
        + [
            pltpu.VMEM((1, LANES), jnp.int32),
            pltpu.VMEM((columns, capacity), jnp.int32),
            pltpu.SemaphoreType.DMA((6,)),
        ],
    )(
        line(rup_x),
        line(rup_y),
        line(rup_mag),
        line(rup_rate),
        line(rup_source),
        relay_sites[0, 0],
    )
    units = rows * LANES // SUBLANES
    sums_shape = (tiles * levels, SUBLANES, LANES)
    own, sums = pl.pallas_call(
        functools.partial(own_kernel, levels),
        out_shape=(
            jax.ShapeDtypeStruct((3 * tiles + 2, LANES), jnp.float32),
            jax.ShapeDtypeStruct(sums_shape, jnp.float32),
        ),
        in_specs=[VMEM] * 6,
        out_specs=(VMEM, VMEM),
        scratch_shapes=[pltpu.VMEM((2 + tiles, units // rows, SUBLANES, LANES), jnp.float32)],
        compiler_params=limit,
    )(
        packed,
        square(site_x),
        square(site_y),
        square(site_amp),
        line(src_sigma),
        line(src_shift),
    )
    groups = [[j * columns + partner(0, d, j) for j in range(rows)] for d in range(columns)]
    ruptures = lax.all_to_all(packed, ("rup", "site"), 0, 0, axis_index_groups=groups, tiled=True)
    heights = 4
    length = tiles * levels
    copy = jax.ShapeDtypeStruct((length + SUBLANES, LANES), jnp.float32)
    copies = pl.pallas_call(
        functools.partial(hazard_kernel, levels),
        out_shape=(copy,) * heights,
        in_specs=[VMEM] * 3,
        out_specs=(VMEM,) * heights,
        scratch_shapes=[
            pltpu.VMEM((2 + tiles, units, SUBLANES, LANES), jnp.float32),
            pltpu.VMEM(sums_shape, jnp.float32),
        ],
        compiler_params=limit,
    )(own, sums, ruptures)
    swap = lambda k: lax.ppermute(copies[k], "rup", [(r, r ^ k) for r in range(rows)])
    east = rows // heights
    merged = pl.pallas_call(
        functools.partial(merge_kernel, heights),
        out_shape=(jax.ShapeDtypeStruct((heights * length + SUBLANES, LANES), jnp.float32),) * east,
        in_specs=[VMEM] * heights,
        out_specs=(VMEM,) * east,
        compiler_params=limit,
    )(*[swap(k) if k else copies[0] for k in FAR_FIRST])
    shift = lambda k: lax.ppermute(
        merged[k], "rup", [(r, r ^ (k * heights)) for r in range(rows)]
    )
    parts = [shift(k) if k else merged[0] for k in FAR_FIRST]
    hazard = pl.pallas_call(
        functools.partial(output_kernel, levels),
        out_shape=jax.ShapeDtypeStruct((levels, sites), jnp.float32),
        in_specs=[VMEM] * east,
        out_specs=VMEM,
        compiler_params=limit,
    )(*parts)
    send = pl.pallas_call(
        functools.partial(relay_kernel, levels, own_sites),
        out_shape=jax.ShapeDtypeStruct((columns, levels, capacity), jnp.float32),
        in_specs=[VMEM] * east,
        out_specs=VMEM,
        scratch_shapes=[pltpu.VMEM((rows * levels, 3 * own_sites), jnp.bfloat16)],
        compiler_params=limit,
    )(*parts)
    curves = lax.all_to_all(send, "site", 0, 0, tiled=True)
    table = jnp.transpose(vulnerability, (1, 2, 0)).reshape(levels * bins, classes)
    slot, split = pl.pallas_call(
        table_kernel,
        out_shape=(
            jax.ShapeDtypeStruct((assets // LANES, LANES), jnp.int32),
            jax.ShapeDtypeStruct((levels * bins, 2 * classes), jnp.bfloat16),
        ),
        in_specs=[VMEM, VMEM, SMEM, VMEM],
        out_specs=(VMEM, VMEM),
        compiler_params=limit,
    )(square(asset_source), square(asset_pick), relay_count.reshape(1, sources), table)
    losses = pl.pallas_call(
        loss_kernel,
        out_shape=jax.ShapeDtypeStruct((bins, assets), jnp.float32),
        in_specs=[VMEM] * 5,
        out_specs=VMEM,
        scratch_shapes=[
            pltpu.VMEM((sources * levels // 2, 6 * LANES), jnp.bfloat16),
            pltpu.VMEM((levels, assets), jnp.float32),
        ],
        compiler_params=limit,
    )(curves, square(asset_source), slot, square(asset_class), split)
    return hazard, losses


def solution(mesh):
    return jax.shard_map(
        functools.partial(per_device, rows=mesh.shape["rup"], columns=mesh.shape["site"]),
        mesh=mesh,
        in_specs=(
            P("site"),
            P("site"),
            P("site"),
            P("rup"),
            P("rup"),
            P("rup"),
            P("rup"),
            P("rup"),
            P(),
            P(),
            P("rup", "site", None, None),
            P("rup", "site", None),
            P(("rup", "site")),
            P(("rup", "site")),
            P(("rup", "site")),
            P(),
        ),
        out_specs=(P(None, "site"), P(None, ("rup", "site"))),
        check_vma=False,
    )
```

```python
import functools
import math

import jax
import jax.numpy as jnp
from jax import lax
from jax.experimental import pallas as pl
from jax.experimental.pallas import tpu as pltpu
from jax.sharding import PartitionSpec as P

LANES = 128
SUBLANES = 8
LIST = 5
FAR_FIRST = (0, 2, 1, 3)
UNROLL = 48
PRODUCTS = 2
VMEM = pl.BlockSpec(memory_space=pltpu.VMEM)
SMEM = pl.BlockSpec(memory_space=pltpu.SMEM)
LEVEL_FIRST = math.log(0.005)
LEVEL_RANGE = math.log(600.0)


def lane_gather(row, index):
    return jnp.take_along_axis(row, index, axis=1, mode="promise_in_bounds")


def partner(row, site, other):
    inner = lambda r: (((r & 3) + 1) >> 1) & 1
    south = lambda r: 2 * inner(r) - (r >> 2)
    z_lo = (site >> 3) ^ inner(row) ^ inner(other)
    y = (((site >> 1) & 3) - south(row) + south(other)) & 3
    core = (site & 1) ^ ((row & 3) >> 1) ^ ((other & 3) >> 1)
    return z_lo * 8 + y * 2 + core


def place():
    return lax.axis_index("rup"), lax.axis_index("site")


def split_in_three(value):
    high = value.astype(jnp.bfloat16)
    rest = value - high.astype(jnp.float32)
    middle = rest.astype(jnp.bfloat16)
    return high, middle, (rest - middle.astype(jnp.float32)).astype(jnp.bfloat16)


def pack_kernel(x_ref, y_ref, mag_ref, rate_ref, source_ref, relay_ref, out_ref):
    row, site = place()
    source = source_ref[...].astype(jnp.float32)
    zero = jnp.zeros((1, LANES), jnp.float32)
    packed = jnp.concatenate(
        [x_ref[...], y_ref[...], mag_ref[...], rate_ref[...], source, zero, zero, zero], axis=0
    )
    for j in range(out_ref.shape[0]):
        out_ref[j] = packed
        wanted = relay_ref[pl.ds(partner(row, site, j), 1), :]
        out_ref[j, LIST : LIST + 1, :] = wanted.astype(jnp.float32)


def wide(row):
    return jnp.broadcast_to(row, (SUBLANES, LANES))


def spreading():
    part = lax.broadcasted_iota(jnp.int32, (4 * SUBLANES, 5 * LANES), 0)
    which = lax.broadcasted_iota(jnp.int32, (4 * SUBLANES, 5 * LANES), 1) >> 7
    chosen = (part < 3 * SUBLANES) & ((part & (SUBLANES - 1)) == which)
    return jnp.where(chosen, 1.0, 0.0).astype(jnp.bfloat16)


def prepare(raw, at, levels, own_ref, spread_out, pre_ref):
    tiles = pre_ref.shape[0] - 2
    units = LANES // SUBLANES
    step = LEVEL_RANGE / (levels - 1)
    index = wide(raw[4:5]).astype(jnp.int32)
    sigma = wide(own_ref[3 * tiles : 3 * tiles + 1, :])
    shift = wide(own_ref[3 * tiles + 1 : 3 * tiles + 2, :])
    inverse = 1.0 / (lane_gather(sigma, index)[0:1] * math.sqrt(2.0))
    base = -1.0 + (raw[2:3] - 6.5) + lane_gather(shift, index)[0:1]
    zero = jnp.zeros((3, LANES), jnp.float32)
    rows = jnp.concatenate([raw[0:2], base, inverse, 0.5 * raw[3:4], zero], axis=0)
    thirds = [third.astype(jnp.float32) for third in split_in_three(rows)]
    stack = jnp.concatenate(thirds + [jnp.zeros_like(rows)], axis=0).astype(jnp.bfloat16)
    columns = lax.dot_general(
        stack, spread_out, (((0,), (0,)), ((), ())), preferred_element_type=jnp.float32
    )
    sites = [[wide(own_ref[i * tiles + t : i * tiles + t + 1, :]) for i in range(3)] for t in range(tiles)]
    for u in range(units):
        x, y, base, inverse, rate = [
            columns[u * SUBLANES : (u + 1) * SUBLANES, p * LANES : (p + 1) * LANES]
            for p in range(5)
        ]
        k = at * units + u
        pre_ref[0, k] = rate
        pre_ref[1, k] = inverse * step
        for t in range(tiles):
            site_x, site_y, amp = sites[t]
            dx = site_x - x
            dy = site_y - y
            median = base + amp - 0.6 * jnp.log((dx * dx + dy * dy + 100.0) * 0.01)
            pre_ref[2 + t, k] = (LEVEL_FIRST - median) * inverse


def tails(first, count, t, levels, pre_ref):
    total = [None] * levels
    for u in range(count):
        rate = pre_ref[0, first + u]
        gap = pre_ref[1, first + u]
        start = pre_ref[2 + t, first + u]
        whole = rate if u == 0 else whole + rate
        for l in range(levels):
            z = z + gap if l % 16 else start + gap * float(l)
            term = rate * lax.erf(z)
            total[l] = term if u == 0 else total[l] + term
    return [whole - part for part in total]


def own_kernel(
    levels, rup_ref, sx_ref, sy_ref, amp_ref, sigma_ref, shift_ref, own_ref, acc_ref, pre_ref
):
    rows = rup_ref.shape[0]
    row = place()[0]
    tiles = sx_ref.shape[0] // rows
    for i, ref in enumerate((sx_ref, sy_ref, amp_ref)):
        own_ref[i * tiles : (i + 1) * tiles, :] = ref[pl.ds(row * tiles, tiles), :]
    sources = sigma_ref.shape[1]
    own_ref[3 * tiles : 3 * tiles + 2, :] = jnp.zeros((2, LANES), jnp.float32)
    own_ref[3 * tiles : 3 * tiles + 1, 0:sources] = sigma_ref[...]
    own_ref[3 * tiles + 1 : 3 * tiles + 2, 0:sources] = shift_ref[...]
    prepare(rup_ref[0], 0, levels, own_ref, spreading(), pre_ref)
    for t in range(tiles):
        sums = tails(0, LANES // SUBLANES, t, levels, pre_ref)
        for l in range(levels):
            acc_ref[t * levels + l] = sums[l]


def hazard_kernel(levels, own_ref, sums_ref, rup_ref, *refs):
    out_refs, pre_ref, acc_ref = refs[:-2], refs[-2], refs[-1]
    blocks = rup_ref.shape[0]
    heights = len(out_refs)
    tiles = out_refs[0].shape[0] // levels
    units = LANES // SUBLANES
    row = place()[0]
    spread_out = spreading()
    acc_ref[...] = sums_ref[...]
    others = blocks - 1
    together = 5

    def prepare_some(g, carry):
        for i in range(together):
            at = g * together + i
            block = (row + 1 + at) & (blocks - 1)
            prepare(rup_ref[block], at, levels, own_ref, spread_out, pre_ref)
        return carry

    lax.fori_loop(0, others // together, prepare_some, 0)
    unroll = UNROLL

    for t in range(tiles):

        def add(g, carry):
            sums = tails(g * unroll, unroll, t, levels, pre_ref)
            for l in range(levels):
                at = t * levels + l
                acc_ref[at] = acc_ref[at] + sums[l]
            return carry

        lax.fori_loop(0, others * units // unroll, add, 0)
    for t in range(tiles):
        for q in range(0, levels, SUBLANES):
            rates = jnp.concatenate(
                [
                    jnp.sum(acc_ref[t * levels + l], axis=0, keepdims=True)
                    for l in range(q, q + SUBLANES)
                ],
                axis=0,
            )
            hazard = 1.0 - jnp.exp(-rates)
            for out_ref in out_refs:
                out_ref[t * levels + q : t * levels + q + SUBLANES, :] = hazard
    for k, out_ref in enumerate(out_refs):
        height = (row & (heights - 1)) ^ k
        lists = [rup_ref[x * heights + height, LIST : LIST + 1, :] for x in range(blocks // heights)]
        lists.append(jnp.zeros((SUBLANES - len(lists), LANES), jnp.float32))
        out_ref[tiles * levels :, :] = jnp.concatenate(lists, axis=0)


def merge_kernel(heights, *refs):
    in_refs, out_refs = refs[:heights], refs[heights:]
    length = in_refs[0].shape[0] - SUBLANES
    row = place()[0]
    for k, out_ref in enumerate(out_refs):
        x = (row >> 2) ^ k
        out_ref[heights * length :, :] = jnp.zeros((SUBLANES, LANES), jnp.float32)
        for flip, in_ref in zip(FAR_FIRST, in_refs):
            height = (row & (heights - 1)) ^ flip
            at = pl.multiple_of(height * length, length)
            out_ref[pl.ds(at, length), :] = in_ref[0:length, :]
            out_ref[pl.ds(heights * length + height, 1), :] = in_ref[pl.ds(length + x, 1), :]


def output_kernel(levels, *refs):
    in_refs, out_ref = refs[:-1], refs[-1]
    row = place()[0]
    tiles = out_ref.shape[1] // (len(in_refs) * LANES)
    for k, in_ref in zip(FAR_FIRST, in_refs):
        x = (row >> 2) ^ k
        for t in range(tiles):
            at = pl.multiple_of((x * tiles + t) * LANES, LANES)
            out_ref[:, pl.ds(at, LANES)] = in_ref[t * levels : (t + 1) * levels, :]


def pick_by_product(lhs_ref, levels, index):
    span = lhs_ref.shape[1] // 3
    blocks = lhs_ref.shape[0] // levels
    width = index.shape[1]
    low = index & (span - 1)
    high = jnp.broadcast_to(index >> (span.bit_length() - 1), (SUBLANES, width))
    match = lax.broadcasted_iota(jnp.int32, (span, width), 0) == low
    onehot = jnp.where(match, 1.0, 0.0).astype(jnp.bfloat16)
    found = jnp.dot(
        lhs_ref[...],
        jnp.concatenate([onehot] * 3, axis=0),
        preferred_element_type=jnp.float32,
    )
    picked = [jnp.zeros((SUBLANES, width), jnp.float32)] * (levels // SUBLANES)
    for b in range(blocks):
        here = high == b
        for q in range(len(picked)):
            at = b * levels + q * SUBLANES
            picked[q] = jnp.where(here, found[at : at + SUBLANES], picked[q])
    return picked


def relay_kernel(levels, span, *refs):
    part_refs, send_ref, lhs_ref = [refs[k] for k in FAR_FIRST], refs[-2], refs[-1]
    parts = len(part_refs)
    heights = (part_refs[0].shape[0] - SUBLANES) * LANES // (levels * span)
    blocks = parts * heights
    groups = levels // SUBLANES
    tiles = span // LANES
    row, site = place()

    def origin(b):
        return ((row >> 2) ^ (b // heights)) * heights + b % heights

    def piece(b, t, first, count):
        at = (b % heights * tiles + t) * levels + first
        return part_refs[b // heights][at : at + count, :]

    def wanted(k):
        at = heights * tiles * levels + k % heights
        return part_refs[k // heights][at : at + 1, :].astype(jnp.int32)

    for b in range(blocks):
        for t in range(tiles):
            thirds = split_in_three(piece(b, t, 0, levels))
            for i in range(3):
                at = i * span + t * LANES
                first = pl.multiple_of(origin(b) * levels, levels)
                lhs_ref[pl.ds(first, levels), at : at + LANES] = thirds[i]

    def by_product(k):
        index = jnp.concatenate([wanted(k + i) for i in range(2)], axis=1)
        picked = pick_by_product(lhs_ref, levels, index)
        for i in range(2):
            owner = partner(origin(k + i), site, row)
            for q in range(groups):
                send_ref[owner, q * SUBLANES : (q + 1) * SUBLANES, :] = picked[q][
                    :, i * LANES : (i + 1) * LANES
                ]

    def by_gather(k):
        index = wide(wanted(k))
        lane = index & (LANES - 1)
        tile = index >> 7
        picked = [jnp.zeros((SUBLANES, LANES), jnp.float32)] * groups
        for c in range(blocks * tiles):
            b, t = c // tiles, c % tiles
            here = tile == origin(b) * tiles + t
            for q in range(groups):
                part = piece(b, t, q * SUBLANES, SUBLANES)
                picked[q] = jnp.where(here, lane_gather(part, lane), picked[q])
        owner = partner(origin(k), site, row)
        for q in range(groups):
            send_ref[owner, q * SUBLANES : (q + 1) * SUBLANES, :] = picked[q]

    products = blocks * 5 // 16
    for i in range(products):
        by_product(2 * i)
        by_gather(2 * products + i)
    for k in range(3 * products, blocks):
        by_gather(k)


def table_kernel(source_ref, pick_ref, count_ref, table_ref, slot_ref, split_ref):
    source = source_ref[...]
    count = jnp.zeros(source.shape, jnp.int32)
    for s in range(count_ref.shape[1]):
        count = jnp.where(source == s, count_ref[0, s], count)
    pick = pick_ref[...]
    quotient = jnp.floor(pick.astype(jnp.float32) / count.astype(jnp.float32)).astype(jnp.int32)
    slot = pick - quotient * count
    slot = jnp.where(slot < 0, slot + count, slot)
    slot_ref[...] = jnp.where(slot >= count, slot - count, slot)
    classes = table_ref.shape[1]
    table = table_ref[...]
    high = table.astype(jnp.bfloat16)
    split_ref[:, 0:classes] = high
    split_ref[:, classes : 2 * classes] = (table - high.astype(jnp.float32)).astype(jnp.bfloat16)


def loss_kernel(
    curves_ref, source_ref, slot_ref, class_ref, split_ref, out_ref, lhs_ref, change_ref
):
    sources, levels, _ = curves_ref.shape
    bins, assets = out_ref.shape
    classes = split_ref.shape[1] // 2
    groups = levels // SUBLANES
    width = 2 * LANES
    for s in range(sources):
        thirds = split_in_three(curves_ref[s])
        for i in range(3):
            at = i * width + (s % 2) * LANES
            lhs_ref[s // 2 * levels : (s // 2 + 1) * levels, at : at + LANES] = thirds[i]

    def by_product(t):
        index = jnp.concatenate(
            [source_ref[i : i + 1, :] * LANES + slot_ref[i : i + 1, :] for i in (2 * t, 2 * t + 1)],
            axis=1,
        )
        return pick_by_product(lhs_ref, levels, index)

    def by_gather(t):
        halves = []
        for i in (2 * t, 2 * t + 1):
            lane = wide(slot_ref[i : i + 1, :])
            which = wide(source_ref[i : i + 1, :])
            half = [jnp.zeros((SUBLANES, LANES), jnp.float32)] * groups
            for s in range(sources):
                here = which == s
                for q in range(groups):
                    part = curves_ref[s, q * SUBLANES : (q + 1) * SUBLANES, :]
                    half[q] = jnp.where(here, lane_gather(part, lane), half[q])
            halves.append(half)
        return [jnp.concatenate([h[q] for h in halves], axis=1) for q in range(groups)]

    for t in range(assets // width):
        curves = jnp.concatenate(by_product(t) if t < PRODUCTS else by_gather(t), axis=0)
        following = jnp.concatenate([curves[1:], jnp.zeros((1, width), jnp.float32)], axis=0)
        change_ref[:, t * width : (t + 1) * width] = curves - following
    for t in range(assets // width):
        across = slice(t * width, (t + 1) * width)
        kinds = jnp.concatenate([class_ref[i : i + 1, :] for i in (2 * t, 2 * t + 1)], axis=1)
        match = lax.broadcasted_iota(jnp.int32, (classes, width), 0) == kinds
        onehot = jnp.where(match, 1.0, 0.0).astype(jnp.bfloat16)
        both = jnp.concatenate([onehot, onehot], axis=0)
        chosen = jnp.dot(split_ref[...], both, preferred_element_type=jnp.float32)
        total = jnp.zeros((bins, width), jnp.float32)
        for l in range(levels):
            part = chosen[l * bins : (l + 1) * bins, :]
            total = total + change_ref[l : l + 1, across] * part
        out_ref[:, across] = total


def per_device(
    site_x,
    site_y,
    site_amp,
    rup_x,
    rup_y,
    rup_mag,
    rup_rate,
    rup_source,
    src_sigma,
    src_shift,
    relay_sites,
    relay_count,
    asset_source,
    asset_pick,
    asset_class,
    vulnerability,
    rows,
    columns,
):
    classes, levels, bins = vulnerability.shape
    sites = site_x.shape[0]
    sources, capacity = relay_sites.shape[2:]
    assets = asset_source.shape[0]
    own_sites = sites // rows
    limit = pltpu.CompilerParams(vmem_limit_bytes=48 * 2**20)

    line = lambda a: a.reshape(1, -1)
    square = lambda a: a.reshape(-1, LANES)
    tiles = own_sites // LANES
    packed = pl.pallas_call(
        pack_kernel,
        out_shape=jax.ShapeDtypeStruct((rows, SUBLANES, LANES), jnp.float32),
        in_specs=[VMEM] * 6,
        out_specs=VMEM,
    )(
        line(rup_x),
        line(rup_y),
        line(rup_mag),
        line(rup_rate),
        line(rup_source),
        relay_sites[0, 0],
    )
    units = rows * LANES // SUBLANES
    sums_shape = (tiles * levels, SUBLANES, LANES)
    own, sums = pl.pallas_call(
        functools.partial(own_kernel, levels),
        out_shape=(
            jax.ShapeDtypeStruct((3 * tiles + 2, LANES), jnp.float32),
            jax.ShapeDtypeStruct(sums_shape, jnp.float32),
        ),
        in_specs=[VMEM] * 6,
        out_specs=(VMEM, VMEM),
        scratch_shapes=[pltpu.VMEM((2 + tiles, units // rows, SUBLANES, LANES), jnp.float32)],
        compiler_params=limit,
    )(
        packed,
        square(site_x),
        square(site_y),
        square(site_amp),
        line(src_sigma),
        line(src_shift),
    )
    groups = [[j * columns + partner(0, d, j) for j in range(rows)] for d in range(columns)]
    ruptures = lax.all_to_all(packed, ("rup", "site"), 0, 0, axis_index_groups=groups, tiled=True)
    heights = 4
    length = tiles * levels
    copy = jax.ShapeDtypeStruct((length + SUBLANES, LANES), jnp.float32)
    copies = pl.pallas_call(
        functools.partial(hazard_kernel, levels),
        out_shape=(copy,) * heights,
        in_specs=[VMEM] * 3,
        out_specs=(VMEM,) * heights,
        scratch_shapes=[
            pltpu.VMEM((2 + tiles, units, SUBLANES, LANES), jnp.float32),
            pltpu.VMEM(sums_shape, jnp.float32),
        ],
        compiler_params=limit,
    )(own, sums, ruptures)
    swap = lambda k: lax.ppermute(copies[k], "rup", [(r, r ^ k) for r in range(rows)])
    east = rows // heights
    merged = pl.pallas_call(
        functools.partial(merge_kernel, heights),
        out_shape=(jax.ShapeDtypeStruct((heights * length + SUBLANES, LANES), jnp.float32),) * east,
        in_specs=[VMEM] * heights,
        out_specs=(VMEM,) * east,
        compiler_params=limit,
    )(*[swap(k) if k else copies[0] for k in FAR_FIRST])
    shift = lambda k: lax.ppermute(
        merged[k], "rup", [(r, r ^ (k * heights)) for r in range(rows)]
    )
    parts = [shift(k) if k else merged[0] for k in FAR_FIRST]
    hazard = pl.pallas_call(
        functools.partial(output_kernel, levels),
        out_shape=jax.ShapeDtypeStruct((levels, sites), jnp.float32),
        in_specs=[VMEM] * east,
        out_specs=VMEM,
        compiler_params=limit,
    )(*parts)
    send = pl.pallas_call(
        functools.partial(relay_kernel, levels, own_sites),
        out_shape=jax.ShapeDtypeStruct((columns, levels, capacity), jnp.float32),
        in_specs=[VMEM] * east,
        out_specs=VMEM,
        scratch_shapes=[pltpu.VMEM((rows * levels, 3 * own_sites), jnp.bfloat16)],
        compiler_params=limit,
    )(*parts)
    curves = lax.all_to_all(send, "site", 0, 0, tiled=True)
    table = jnp.transpose(vulnerability, (1, 2, 0)).reshape(levels * bins, classes)
    slot, split = pl.pallas_call(
        table_kernel,
        out_shape=(
            jax.ShapeDtypeStruct((assets // LANES, LANES), jnp.int32),
            jax.ShapeDtypeStruct((levels * bins, 2 * classes), jnp.bfloat16),
        ),
        in_specs=[VMEM, VMEM, SMEM, VMEM],
        out_specs=(VMEM, VMEM),
        compiler_params=limit,
    )(square(asset_source), square(asset_pick), relay_count.reshape(1, sources), table)
    losses = pl.pallas_call(
        loss_kernel,
        out_shape=jax.ShapeDtypeStruct((bins, assets), jnp.float32),
        in_specs=[VMEM] * 5,
        out_specs=VMEM,
        scratch_shapes=[
            pltpu.VMEM((sources * levels // 2, 6 * LANES), jnp.bfloat16),
            pltpu.VMEM((levels, assets), jnp.float32),
        ],
        compiler_params=limit,
    )(curves, square(asset_source), slot, square(asset_class), split)
    return hazard, losses


def solution(mesh):
    return jax.shard_map(
        functools.partial(per_device, rows=mesh.shape["rup"], columns=mesh.shape["site"]),
        mesh=mesh,
        in_specs=(
            P("site"),
            P("site"),
            P("site"),
            P("rup"),
            P("rup"),
            P("rup"),
            P("rup"),
            P("rup"),
            P(),
            P(),
            P("rup", "site", None, None),
            P("rup", "site", None),
            P(("rup", "site")),
            P(("rup", "site")),
            P(("rup", "site")),
            P(),
        ),
        out_specs=(P(None, "site"), P(None, ("rup", "site"))),
        check_vma=False,
    )
```
